256 devices in a mesh: stream: 32 (over z, x_hi, core), span: 8 (over y, x_lo).
Axes of the slice: x: 4 (x_hi: 2, x_lo: 2; x = x_hi * 2 + x_lo), y: 4, z: 8, core: 2. Of those that a mesh axis runs over, the one named last changes fastest.
Arguments:
- adjoint: bfloat16 [192, 128, 128, 128], P(None, 'stream', 'span'), may hold values from -6 to 6
- velocity: bfloat16 [192, 128, 128, 128], P(None, 'stream', 'span'), may hold values from -6 to 6
- density: float32 [128, 128, 128], P('stream', 'span'), may hold values from 0 to 1
- metric: float32 [128, 128, 128], P('stream', 'span'), may hold values from 0.5 to 2
- orientation: int32 [6, 128, 128, 128], P(None, 'stream', 'span'), may hold values from 0 to 1
- design_ids: int32 [128, 128, 128], P('stream', 'span'), may hold values from 0 to 4
- volume_block: bfloat16 [192, 192], replicated, may hold values from -0.4375 to 0.4375
- face_trace: bfloat16 [6, 48, 192], replicated, may hold values from -0.4375 to 0.4375
- face_lift: bfloat16 [6, 192, 48], replicated, may hold values from -0.875 to 0.875
Outputs:
- residual: bfloat16 [192, 128, 128, 128], P(None, 'stream', 'span')
- filtered: float32 [128, 128, 128], P('stream', 'span')
- volumes: float32 [4], replicated
The draws below stay inside these ranges and needn't reach their ends.
All inputs are finite; a program needn't handle non-finite values.
Results may differ from the reference program's by a relative error of at most 0.0043.
Values may be sent and summed in bfloat16 or wider, within the bound.
A program may use at most 128 MiB of HBM per device.

```python
import math
import jax
import jax.numpy as jnp
from jax import lax

DOFS = 192
TRACE = 48
FACES = 6
GROUPS = 4
CX = 4
CY = 16
NZ = 128
NX = 128
NY = 128


def plant(drawn, own_key, smallest, top_value):
    longest = drawn.shape.index(max(drawn.shape))
    spots = []
    for shift in (0, 1):
        where = [jax.random.randint(jax.random.fold_in(own_key, axis), (), 0, length) for axis, length in enumerate(drawn.shape)]
        where[longest] = (where[longest] + shift) % drawn.shape[longest]
        spots.append(tuple(where))
    return drawn.at[spots[0]].set(smallest).at[spots[1]].set(top_value)


def levels(stream_key, extent, shards, least, top_value):
    loudness, own = 1.0, jax.random.fold_in(stream_key, 6)
    for position, blocks in shards:
        draws = jnp.exp(jax.random.uniform(jax.random.fold_in(own, position), (blocks,), jnp.float32, least / len(shards), top_value / len(shards)))
        loudness = loudness * jnp.repeat(draws, extent[position] // blocks).reshape([-1 if axis == position else 1 for axis in range(len(extent))])
    return loudness


def gaussian(key, dims, spread, limit, cuts=(), kind=jnp.bfloat16):
    result = jax.random.normal(key, dims, jnp.float32) * spread
    if len(cuts) > 0:
        result = levels(key, dims, cuts, -0.22, 0.18) * result
    return jnp.clip(result, min=-limit, max=limit).astype(kind)


def setup_inputs(seed: int = 0) -> dict:
    key_list = jax.random.split(jax.random.key(seed), 10)
    return {
        "adjoint": gaussian(key_list[0], (DOFS, NX, NY, NZ), 1.0, 6.0, ((1, 32), (2, 8))),
        "velocity": gaussian(key_list[1], (DOFS, NX, NY, NZ), 1.0, 6.0, ((1, 32), (2, 8))),
        "density": jnp.clip(1.0 * jax.random.uniform(key_list[2], (NX, NY, NZ), jnp.float32) ** levels(key_list[2], (NX, NY, NZ), ((0, 32), (1, 8)), -0.2, 0.2), 0.0, 1.0),
        "metric": jnp.clip(jnp.exp(math.log(2.0) - 1.3862944 * jax.random.uniform(key_list[3], (NX, NY, NZ), jnp.float32) ** levels(key_list[3], (NX, NY, NZ), ((0, 32), (1, 8)), -0.2, 0.2)), 0.5, 2.0),
        "orientation": plant(jax.random.randint(key_list[4], (FACES, NX, NY, NZ), 0, 2), jax.random.fold_in(key_list[4], 1), 0, 1).astype(jnp.int32),
        "design_ids": plant(jax.random.randint(key_list[5], (NX, NY, NZ), 0, GROUPS + 1), jax.random.fold_in(key_list[5], 1), 0, GROUPS).astype(jnp.int32),
        "volume_block": gaussian(key_list[6], (DOFS, DOFS), DOFS ** -0.5, 0.4375),
        "face_trace": gaussian(key_list[7], (FACES, TRACE, DOFS), DOFS ** -0.5, 0.4375),
        "face_lift": gaussian(key_list[8], (FACES, DOFS, TRACE), TRACE ** -0.5, 0.875),
    }


sens_scale = 0.03125
filter_beta = 0.5


def shift_axis(field, axis, offset):
    zeros = jnp.zeros_like(lax.slice_in_dim(field, 0, 1, axis=axis))
    size = field.shape[axis]
    if offset < 0:
        return jnp.concatenate([zeros, lax.slice_in_dim(field, 0, size - 1, axis=axis)], axis=axis)
    return jnp.concatenate([lax.slice_in_dim(field, 1, size, axis=axis), zeros], axis=axis)


def reference(adjoint, velocity, density, metric, orientation, design_ids, volume_block, face_trace, face_lift):
    volume_wide = volume_block.astype(jnp.float32)
    trace_wide = face_trace.astype(jnp.float32)
    lift_wide = face_lift.astype(jnp.float32)

    def slab(index):
        before = (index - 1 + NX) % NX
        after = (index + 1) % NX
        center = lax.dynamic_index_in_dim(adjoint, index, 1, keepdims=False).astype(jnp.float32)
        lower_x = lax.dynamic_index_in_dim(adjoint, before, 1, keepdims=False).astype(jnp.float32)
        upper_x = lax.dynamic_index_in_dim(adjoint, after, 1, keepdims=False).astype(jnp.float32)
        speed = lax.dynamic_index_in_dim(velocity, index, 1, keepdims=False).astype(jnp.float32)
        rho = lax.dynamic_index_in_dim(density, index, 0, keepdims=False)
        scale = lax.dynamic_index_in_dim(metric, index, 0, keepdims=False)
        codes = lax.dynamic_index_in_dim(orientation, index, 1, keepdims=False)
        groups = lax.dynamic_index_in_dim(design_ids, index, 0, keepdims=False)
        alpha = 2.0 * (1.0 - rho) / (1.0 + rho)
        slope = -4.0 / ((1.0 + rho) * (1.0 + rho))
        total = scale[None] * (jnp.einsum("ij,iyz->jyz", volume_wide, center) + alpha[None] * center)
        neighbours = [lower_x, upper_x, shift_axis(center, 1, -1), shift_axis(center, 1, 1),
                      shift_axis(center, 2, -1), shift_axis(center, 2, 1)]
        for face in range(6):
            signs = 1.0 - 2.0 * codes[face].astype(jnp.float32)
            values = jnp.einsum("ti,iyz->tyz", trace_wide[face], neighbours[face]).astype(jnp.bfloat16).astype(jnp.float32)
            total = total + signs[None] * jnp.einsum("jt,tyz->jyz", lift_wide[face], values)
        live = (groups > 0).astype(jnp.float32)
        inner = jnp.sum(speed * center, axis=0)
        sensitivity = (live * slope * scale * inner * sens_scale).astype(jnp.bfloat16)
        return total.astype(jnp.bfloat16), sensitivity

    stacked, sensitivity = lax.map(slab, jnp.arange(NX, dtype=jnp.int32))
    residual = jnp.transpose(stacked, (1, 0, 2, 3))
    sens = sensitivity.astype(jnp.float32)
    beside_all = jnp.roll(sens, 1, axis=0) + jnp.roll(sens, -1, axis=0)
    beside_all = beside_all + shift_axis(sens, 1, -1) + shift_axis(sens, 1, 1)
    beside_all = beside_all + shift_axis(sens, 2, -1) + shift_axis(sens, 2, 1)
    filtered = (sens + filter_beta * beside_all) / (1.0 + 6.0 * filter_beta)
    weighted = density * metric
    parts = []
    for group in range(GROUPS):
        parts.append(jnp.sum(jnp.where(design_ids == group + 1, weighted, jnp.float32(0.0))))
    volumes = jnp.stack(parts) / jnp.float32(CX * CY * NZ)
    return residual, filtered, volumes
```

```python
import functools

import jax
import jax.numpy as jnp
from jax import lax
from jax.experimental import pallas as pl
from jax.experimental.pallas import tpu as pltpu
from jax.sharding import PartitionSpec as P

MESH = pl.DeviceIdType.MESH
F32 = jnp.float32
BF16 = jnp.bfloat16
GROUPS = 4
SENS_SCALE = 0.03125
FILTER_BETA = 0.5
ROWS = 48
CHUNK = 4


def shift_rows(field, first, up):
    row = lax.broadcasted_iota(jnp.int32, field.shape, 0)
    edge = field.shape[0] - 1 if up else 0
    moved = pltpu.roll(field, field.shape[0] - 1 if up else 1, 0)
    return jnp.where(row == edge, first, moved)


def shift_lanes(field, up):
    lane = lax.broadcasted_iota(jnp.int32, field.shape, field.ndim - 1)
    edge = 127 if up else 0
    moved = pltpu.roll(field, 127 if up else 1, field.ndim - 1)
    return jnp.where(lane == edge, jnp.zeros_like(field), moved)


def first_kernel(
    n_stream, n_span, remote,
    adj_hbm, vel_hbm, den_hbm, met_hbm, ids_hbm, vol_hbm, trace_hbm,
    base, tx0, tx1, ty2, ty3, tz4, tz5, sens, sx_lo, sx_hi, sy_lo, sy_hi, vol_out,
    adj, vel, den, met, ids, vol, weights, send_lo, send_hi, slots_a, slots_b, part_a, part_b,
    in_sem, vel_sem, small_sem, halo_send, halo_recv, a_send, a_recv, b_send, b_recv,
):
    cx = adj.shape[1]
    stream, span = lax.axis_index("stream"), lax.axis_index("span")

    if remote:
        barrier = pltpu.get_barrier_semaphore()

        def greet_span(d, _):
            pl.semaphore_signal(barrier, inc=1, device_id=(stream, lax.rem(span + d, n_span)), device_id_type=MESH)
            return 0

        def greet_stream(d, _):
            pl.semaphore_signal(barrier, inc=1, device_id=(lax.rem(stream + d, n_stream), span), device_id_type=MESH)
            return 0

    trace_copy = pltpu.make_async_copy(trace_hbm, weights.at[pl.ds(192, 288)], small_sem.at[0])
    vol_copy = pltpu.make_async_copy(vol_hbm, vol, small_sem.at[1])
    den_copy = pltpu.make_async_copy(den_hbm, den, small_sem.at[2])
    met_copy = pltpu.make_async_copy(met_hbm, met, small_sem.at[3])
    ids_copy = pltpu.make_async_copy(ids_hbm, ids, small_sem.at[4])

    def adj_copy(x):
        return pltpu.make_async_copy(adj_hbm.at[:, x], adj.at[:, x], in_sem.at[x])

    def vel_copy(x):
        return pltpu.make_async_copy(vel_hbm.at[:, x], vel.at[:, x], vel_sem.at[x])

    vol_copy.start()
    trace_copy.start()
    adj_copy(0).start()
    met_copy.start()
    den_copy.start()
    adj_copy(cx - 1).start()
    ids_copy.start()
    for x in range(1, cx - 1):
        adj_copy(x).start()
    for x in range(cx):
        vel_copy(x * (cx - 1) % cx).start()
    if remote:
        lax.fori_loop(1, n_span, greet_span, 0)
        lax.fori_loop(1, n_stream, greet_stream, 0)

    vol_copy.wait()
    weights[0:192, :] = vol[...].T
    trace_copy.wait()
    met_copy.wait()
    den_copy.wait()
    ids_copy.wait()

    if remote:
        left, right = lax.rem(stream + n_stream - 1, n_stream), lax.rem(stream + 1, n_stream)
        x_down = pltpu.make_async_remote_copy(
            src_ref=tx1.at[0], dst_ref=tx1.at[cx], send_sem=halo_send.at[0], recv_sem=halo_recv.at[0],
            device_id=(left, span), device_id_type=MESH)
        x_up = pltpu.make_async_remote_copy(
            src_ref=tx0.at[cx], dst_ref=tx0.at[0], send_sem=halo_send.at[1], recv_sem=halo_recv.at[1],
            device_id=(right, span), device_id_type=MESH)
        below, above = jnp.maximum(span - 1, 0), jnp.minimum(span + 1, n_span - 1)
        y_down = pltpu.make_async_remote_copy(
            src_ref=ty3.at[:, :, pl.ds(0, 128)], dst_ref=ty3.at[:, :, pl.ds(2048, 128)],
            send_sem=halo_send.at[2], recv_sem=halo_recv.at[2],
            device_id=(stream, below), device_id_type=MESH)
        y_up = pltpu.make_async_remote_copy(
            src_ref=ty2.at[:, :, pl.ds(2048, 128)], dst_ref=ty2.at[:, :, pl.ds(0, 128)],
            send_sem=halo_send.at[3], recv_sem=halo_recv.at[3],
            device_id=(stream, above), device_id_type=MESH)
        s_down = pltpu.make_async_remote_copy(
            src_ref=sens.at[0], dst_ref=sx_hi, send_sem=halo_send.at[4], recv_sem=halo_recv.at[4],
            device_id=(left, span), device_id_type=MESH)
        s_up = pltpu.make_async_remote_copy(
            src_ref=sens.at[cx - 1], dst_ref=sx_lo, send_sem=halo_send.at[5], recv_sem=halo_recv.at[5],
            device_id=(right, span), device_id_type=MESH)
        q_down = pltpu.make_async_remote_copy(
            src_ref=send_lo, dst_ref=sy_hi, send_sem=halo_send.at[6], recv_sem=halo_recv.at[6],
            device_id=(stream, below), device_id_type=MESH)
        q_up = pltpu.make_async_remote_copy(
            src_ref=send_hi, dst_ref=sy_lo, send_sem=halo_send.at[7], recv_sem=halo_recv.at[7],
            device_id=(stream, above), device_id_type=MESH)

        def a_copy(d):
            other = lax.rem(span + d, n_span)
            return pltpu.make_async_remote_copy(
                src_ref=part_a, dst_ref=slots_a.at[span], send_sem=a_send.at[d], recv_sem=a_recv.at[span],
                device_id=(stream, other), device_id_type=MESH)

        def b_copy(d):
            other = lax.rem(stream + d, n_stream)
            return pltpu.make_async_remote_copy(
                src_ref=part_b, dst_ref=slots_b.at[stream], send_sem=b_send.at[d], recv_sem=b_recv.at[stream],
                device_id=(other, span), device_id_type=MESH)

        def a_from(d):
            other = lax.rem(span + d, n_span)
            return pltpu.make_async_remote_copy(
                src_ref=part_a, dst_ref=slots_a.at[other], send_sem=a_send.at[d], recv_sem=a_recv.at[other],
                device_id=(stream, other), device_id_type=MESH)

        def b_from(d):
            other = lax.rem(stream + d, n_stream)
            return pltpu.make_async_remote_copy(
                src_ref=part_b, dst_ref=slots_b.at[other], send_sem=b_send.at[d], recv_sem=b_recv.at[other],
                device_id=(other, span), device_id_type=MESH)

    weighted = den[...] * met[...]
    lane = lax.broadcasted_iota(jnp.int32, (1, 128), 1)
    row = jnp.zeros((1, 128), F32)
    for g in range(GROUPS):
        mine = jnp.sum(jnp.where(ids[...] == g + 1, weighted, 0.0), axis=0)
        mine = jnp.sum(jnp.sum(mine, axis=0, keepdims=True), axis=1, keepdims=True)
        row = row + jnp.where(lane == g, mine, 0.0)
    part_a[...] = row
    if remote:
        slots_a[span] = row

    def slab(i, _):
        x = lax.rem(i * (cx - 1), cx)
        adj_copy(x).wait()
        rho, scale = den[x], met[x]
        alpha = 2.0 * (1.0 - rho) / (1.0 + rho)
        for y0 in range(0, 16, CHUNK):
            turned = jnp.swapaxes(adj[:, x], 0, 1)
            cols = jnp.concatenate([turned[y0 + j] for j in range(CHUNK)], axis=1)
            got = jnp.dot(weights[...], cols, preferred_element_type=F32)
            for j in range(CHUNK):
                y = y0 + j
                own = turned[y].astype(F32)
                total = got[0:192, j * 128 : (j + 1) * 128]
                base[x, y] = scale[y : y + 1] * (total + alpha[y : y + 1] * own)
            t = got[192:480]
            lanes = slice(y0 * 128, (y0 + CHUNK) * 128)
            later = slice(y0 * 128 + 128, (y0 + CHUNK) * 128 + 128)
            tx0[x + 1, :, lanes] = t[0:48].astype(BF16)
            tx1[x, :, lanes] = t[48:96].astype(BF16)
            ty2[x, :, later] = t[96:144].astype(BF16)
            ty3[x, :, lanes] = t[144:192].astype(BF16)
            for j in range(CHUNK):
                at = slice((y0 + j) * 128, (y0 + j + 1) * 128)
                tz4[x, :, at] = shift_lanes(t[192:240, j * 128 : (j + 1) * 128], False).astype(BF16)
                tz5[x, :, at] = shift_lanes(t[240:288, j * 128 : (j + 1) * 128], True).astype(BF16)

        if remote:
            @pl.when(i == 0)
            def _():
                pl.semaphore_wait(barrier, n_span + n_stream - 2)
                x_down.start()

            @pl.when(i == 1)
            def _():
                x_up.start()

        return 0

    lax.fori_loop(0, cx, slab, 0)
    if remote:
        @pl.when(span > 0)
        def _():
            y_down.start()

        @pl.when(span < n_span - 1)
        def _():
            y_up.start()

        def send_a(d, _):
            a_copy(d).start()
            return 0

        lax.fori_loop(1, n_span, send_a, 0)

    def sensing(i, _):
        x = lax.rem(i * (cx - 1), cx)
        vel_copy(x).wait()
        inner = jnp.zeros((16, 128), F32)
        for c in range(0, 192, 16):
            inner = inner + jnp.sum(adj[c : c + 16, x].astype(F32) * vel[c : c + 16, x].astype(F32), axis=0)
        rho, scale = den[x], met[x]
        slope = -4.0 / ((1.0 + rho) * (1.0 + rho))
        live = jnp.where(ids[x] > 0, 1.0, 0.0)
        value = (live * slope * scale * inner * SENS_SCALE).astype(BF16).astype(F32)
        sens[x] = value
        send_lo[pl.ds(x, 1)] = value[0:1]
        send_hi[pl.ds(x, 1)] = value[15:16]
        return 0

    lax.fori_loop(0, cx, sensing, 0)

    if remote:
        s_down.start()
        s_up.start()

        @pl.when(span > 0)
        def _():
            q_down.start()

        @pl.when(span < n_span - 1)
        def _():
            q_up.start()

        def got_a(d, _):
            a_from(d).wait_recv()
            return 0

        lax.fori_loop(1, n_span, got_a, 0)
        total = slots_a[0]
        for s in range(1, n_span):
            total = total + slots_a[s]
        part_b[...] = total
        slots_b[stream] = total

        def send_b(d, _):
            b_copy(d).start()
            return 0

        lax.fori_loop(1, n_stream, send_b, 0)

    @pl.when(span == 0)
    def _():
        for x in range(cx):
            ty2[x, :, 0:128] = jnp.zeros((ROWS, 128), BF16)
        sy_lo[...] = jnp.zeros_like(sy_lo)

    @pl.when(span == n_span - 1)
    def _():
        for x in range(cx):
            ty3[x, :, 2048:2176] = jnp.zeros((ROWS, 128), BF16)
        sy_hi[...] = jnp.zeros_like(sy_hi)

    if remote:
        def got_b(d, _):
            b_from(d).wait_recv()
            return 0

        lax.fori_loop(1, n_stream, got_b, 0)
        volumes = slots_b[0]
        for s in range(1, n_stream):
            volumes = volumes + slots_b[s]
        vol_out[...] = volumes * (1.0 / (den.shape[0] * den.shape[1] * den.shape[2]))

        def sent_a(d, _):
            a_copy(d).wait_send()
            return 0

        def sent_b(d, _):
            b_copy(d).wait_send()
            return 0

        lax.fori_loop(1, n_span, sent_a, 0)
        lax.fori_loop(1, n_stream, sent_b, 0)

        @pl.when(span > 0)
        def _():
            y_down.wait_send()
            q_down.wait_send()
            y_up.wait_recv()
            q_up.wait_recv()

        @pl.when(span < n_span - 1)
        def _():
            y_up.wait_send()
            q_up.wait_send()
            y_down.wait_recv()
            q_down.wait_recv()

        s_down.wait()
        s_up.wait()
        x_down.wait()
        x_up.wait()
    else:
        vol_out[...] = part_a[...]
        for r in (sx_lo, sx_hi, sy_lo, sy_hi):
            r[...] = jnp.zeros_like(r)


def second_kernel(
    orient_hbm, lift_hbm, base, tx0, tx1, ty2, ty3, tz4, tz5, sens, sx_lo, sx_hi, sy_lo, sy_hi, vol_in,
    res_hbm, filt, vol_out,
    orient, lift, weights, sign, turned, held, in_sem, out_sem,
):
    cx = orient.shape[1]
    orient_copy = pltpu.make_async_copy(orient_hbm, orient, in_sem.at[0])
    lift_copy = pltpu.make_async_copy(lift_hbm, lift, in_sem.at[1])
    orient_copy.start()
    lift_copy.start()

    for x in range(cx):
        own = sens[x]
        below_x = sx_lo[...] if x == 0 else sens[x - 1]
        above_x = sx_hi[...] if x == cx - 1 else sens[x + 1]
        beside = below_x + above_x
        beside = beside + shift_rows(own, sy_lo[x : x + 1], False) + shift_rows(own, sy_hi[x : x + 1], True)
        beside = beside + shift_lanes(own, False) + shift_lanes(own, True)
        filt[x] = (own + FILTER_BETA * beside) / (1.0 + 6.0 * FILTER_BETA)
    for g in range(GROUPS):
        vol_out[g] = vol_in[0, g]

    lift_copy.wait()
    weights[...] = lift[...].T
    orient_copy.wait()
    sign[...] = 1.0 - 2.0 * orient[...].astype(F32)

    def res_copy(x):
        return pltpu.make_async_copy(held.at[x], res_hbm.at[:, x], out_sem.at[x])

    def slab(x, _):
        for y0 in range(0, 16, CHUNK):
            lanes = slice(y0 * 128, (y0 + CHUNK) * 128)
            later = slice(y0 * 128 + 128, (y0 + CHUNK) * 128 + 128)
            faces = (tx0[x, :, lanes], tx1[x + 1, :, lanes], ty2[x, :, lanes], ty3[x, :, later], tz4[x, :, lanes], tz5[x, :, lanes])
            parts = []
            for k in range(6):
                rows = [jnp.broadcast_to(sign[k, x, y0 + j : y0 + j + 1], (ROWS, 128)) for j in range(CHUNK)]
                parts.append(faces[k] * jnp.concatenate(rows, axis=1).astype(BF16))
            lifted = jnp.dot(weights[...], jnp.concatenate(parts, axis=0), preferred_element_type=F32)
            for j in range(CHUNK):
                turned[y0 + j] = (base[x, y0 + j] + lifted[:, j * 128 : (j + 1) * 128]).astype(BF16)
        held[x] = jnp.swapaxes(turned[...], 0, 1)
        res_copy(x).start()
        return 0

    lax.fori_loop(0, cx, slab, 0)
    for x in range(cx):
        res_copy(x).wait()


def in_hbm(array):
    return pltpu.with_memory_space_constraint(array, pltpu.HBM)


def shards(
    n_stream, n_span, remote,
    adjoint, velocity, density, metric, orientation, design_ids, volume_block, face_trace, face_lift
):
    cx = adjoint.shape[1]
    any_spec = pl.BlockSpec(memory_space=pltpu.HBM)
    vmem_spec = pl.BlockSpec(memory_space=pltpu.VMEM)
    mids = [
        ((cx, 16, 192, 128), F32),
        ((cx + 1, ROWS, 2048), BF16),
        ((cx + 1, ROWS, 2048), BF16),
        ((cx, ROWS, 2176), BF16),
        ((cx, ROWS, 2176), BF16),
        ((cx, ROWS, 2048), BF16),
        ((cx, ROWS, 2048), BF16),
        ((cx, 16, 128), F32),
        ((16, 128), F32),
        ((16, 128), F32),
        ((8, 128), F32),
        ((8, 128), F32),
        ((1, 128), F32),
    ]
    dma = pltpu.SemaphoreType.DMA
    whole = (adjoint, velocity, density, metric, design_ids, volume_block, face_trace.reshape(288, 192))
    lift_rows = jnp.swapaxes(face_lift, 1, 2).reshape(288, 192)
    whole, (orientation, lift_rows) = jax.tree.map(in_hbm, (whole, (orientation, lift_rows)))
    mid = pl.pallas_call(
        functools.partial(first_kernel, n_stream, n_span, remote),
        out_shape=[pltpu.VMEM(s, d) for s, d in mids],
        in_specs=[any_spec] * 7,
        out_specs=[vmem_spec] * len(mids),
        scratch_shapes=[
            pltpu.VMEM((192, cx, 16, 128), BF16),
            pltpu.VMEM((192, cx, 16, 128), BF16),
            pltpu.VMEM((cx, 16, 128), F32),
            pltpu.VMEM((cx, 16, 128), F32),
            pltpu.VMEM((cx, 16, 128), jnp.int32),
            pltpu.VMEM((192, 192), BF16),
            pltpu.VMEM((480, 192), BF16),
            pltpu.VMEM((8, 128), F32),
            pltpu.VMEM((8, 128), F32),
            pltpu.VMEM((n_span, 1, 128), F32),
            pltpu.VMEM((n_stream, 1, 128), F32),
            pltpu.VMEM((1, 128), F32),
            pltpu.VMEM((1, 128), F32),
            dma((cx,)), dma((cx,)), dma((5,)), dma((8,)), dma((8,)),
            dma((n_span,)), dma((n_span,)), dma((n_stream,)), dma((n_stream,)),
        ],
        compiler_params=pltpu.CompilerParams(
            collective_id=0 if remote else None, has_side_effects=True, vmem_limit_bytes=24 * 2**20
        ),
    )(*whole)
    mid = [pltpu.with_memory_space_constraint(m, pltpu.VMEM) for m in mid]
    return pl.pallas_call(
        second_kernel,
        out_shape=[
            jax.ShapeDtypeStruct(adjoint.shape, BF16),
            jax.ShapeDtypeStruct((cx, 16, 128), F32),
            jax.ShapeDtypeStruct((GROUPS,), F32),
        ],
        in_specs=[any_spec] * 2 + [vmem_spec] * len(mids),
        out_specs=[any_spec, vmem_spec, pl.BlockSpec(memory_space=pltpu.SMEM)],
        scratch_shapes=[
            pltpu.VMEM((6, cx, 16, 128), jnp.int32),
            pltpu.VMEM((288, 192), BF16),
            pltpu.VMEM((192, 288), BF16),
            pltpu.VMEM((6, cx, 16, 128), F32),
            pltpu.VMEM((16, 192, 128), BF16),
            pltpu.VMEM((cx, 192, 16, 128), BF16),
            dma((2,)), dma((cx,)),
        ],
        compiler_params=pltpu.CompilerParams(vmem_limit_bytes=24 * 2**20),
    )(orientation, lift_rows, *mid)


def solution(mesh, remote=True):
    cells = P("stream", "span", None)
    dofs = P(None, "stream", "span", None)
    return jax.shard_map(
        functools.partial(shards, mesh.shape["stream"], mesh.shape["span"], remote),
        mesh=mesh,
        in_specs=(dofs, dofs, cells, cells, dofs, cells, P(), P(), P()),
        out_specs=(dofs, cells, P()),
        check_vma=False,
    )
```

```python
import functools

import jax
import jax.numpy as jnp
from jax import lax
from jax.experimental import pallas as pl
from jax.experimental.pallas import tpu as pltpu
from jax.sharding import PartitionSpec as P

MESH = pl.DeviceIdType.MESH
F32 = jnp.float32
BF16 = jnp.bfloat16
GROUPS = 4
SENS_SCALE = 0.03125
FILTER_BETA = 0.5
ROWS = 48
CHUNK = 4
PLANE = 4


def shift_rows(field, first, up):
    row = lax.broadcasted_iota(jnp.int32, field.shape, 0)
    edge = field.shape[0] - 1 if up else 0
    moved = pltpu.roll(field, field.shape[0] - 1 if up else 1, 0)
    return jnp.where(row == edge, first, moved)


def shift_lanes(field, up):
    lane = lax.broadcasted_iota(jnp.int32, field.shape, field.ndim - 1)
    edge = 127 if up else 0
    moved = pltpu.roll(field, 127 if up else 1, field.ndim - 1)
    return jnp.where(lane == edge, jnp.zeros_like(field), moved)


def wait_for_copies(slots, count, send_sem, recv_sem, device):
    return pltpu.make_async_remote_copy(
        src_ref=slots.at[pl.ds(0, count)], dst_ref=slots.at[pl.ds(0, count)],
        send_sem=send_sem, recv_sem=recv_sem, device_id=device, device_id_type=MESH)


def first_kernel(
    n_stream, n_span, remote,
    adj_hbm, vel_hbm, den_hbm, met_hbm, ids_hbm, orient_hbm, vol_hbm, trace_hbm, lift_hbm,
    held, filt, vol_out,
    adj, vel, den, met, ids, orient, vol, lift, weights, lift_weights, sign, turned, back, base,
    tx0, tx1, ty2, ty3, tz4, tz5, sens, sx_lo, sx_hi, sy_lo, sy_hi,
    send_lo, send_hi, slots_a, slots_b, part_a, part_b,
    in_sem, vel_sem, small_sem, halo_send, halo_recv, vol_send, vol_recv,
):
    cx = adj.shape[1]
    stream, span = lax.axis_index("stream"), lax.axis_index("span")
    left, right = lax.rem(stream + n_stream - 1, n_stream), lax.rem(stream + 1, n_stream)
    below, above = jnp.maximum(span - 1, 0), jnp.minimum(span + 1, n_span - 1)
    n_plane = PLANE * n_span
    n_line = n_stream // PLANE
    line, seat = stream // PLANE, lax.rem(stream, PLANE)
    spot = seat * n_span + span

    def in_plane(d):
        other = lax.rem(spot + d, n_plane)
        return (line * PLANE + other // n_span, lax.rem(other, n_span))

    def in_line(d):
        return (lax.rem(line + d, n_line) * PLANE + seat, span)

    def adj_copy(x):
        return pltpu.make_async_copy(adj_hbm.at[:, x], adj.at[:, x], in_sem.at[x])

    def vel_copy(x):
        return pltpu.make_async_copy(vel_hbm.at[:, x], vel.at[:, x], vel_sem.at[x])

    small = [
        pltpu.make_async_copy(a, b, small_sem.at[i])
        for i, (a, b) in enumerate((
            (vol_hbm, vol), (trace_hbm, weights.at[pl.ds(192, 288)]), (den_hbm, den), (met_hbm, met),
            (ids_hbm, ids), (orient_hbm, orient), (lift_hbm, lift)))
    ]
    for c in small[:5]:
        c.start()
    adj_copy(0).start()
    adj_copy(cx - 1).start()
    vel_copy(0).start()
    adj_copy(2).start()
    vel_copy(cx - 1).start()
    adj_copy(1).start()
    vel_copy(2).start()
    vel_copy(1).start()
    for c in small[5:]:
        c.start()

    if remote:
        barrier = pltpu.get_barrier_semaphore()

        def greet(device):
            pl.semaphore_signal(barrier, inc=1, device_id=device, device_id_type=MESH)

        def greet_plane(d, _):
            greet(in_plane(d))
            return 0

        def greet_line(d, _):
            greet(in_line(d))
            return 0

        greet((left, span))
        greet((right, span))
        lax.fori_loop(1, n_plane, greet_plane, 0)
        lax.fori_loop(1, n_line, greet_line, 0)

        def halo(i, src, dst, device):
            return pltpu.make_async_remote_copy(
                src_ref=src, dst_ref=dst, send_sem=halo_send.at[i], recv_sem=halo_recv.at[i],
                device_id=device, device_id_type=MESH)

        x_down = halo(0, tx1.at[0], tx1.at[cx], (left, span))
        x_up = halo(1, tx0.at[cx], tx0.at[0], (right, span))
        y_down = halo(2, ty3.at[:, :, pl.ds(0, 128)], ty3.at[:, :, pl.ds(2048, 128)], (stream, below))
        y_up = halo(3, ty2.at[:, :, pl.ds(2048, 128)], ty2.at[:, :, pl.ds(0, 128)], (stream, above))
        s_down = halo(4, sens.at[0], sx_hi, (left, span))
        s_up = halo(5, sens.at[cx - 1], sx_lo, (right, span))
        q_down = halo(6, send_lo, sy_hi, (stream, below))
        q_up = halo(7, send_hi, sy_lo, (stream, above))

        def send_a(d, _):
            pltpu.make_async_remote_copy(
                src_ref=part_a, dst_ref=slots_a.at[spot], send_sem=vol_send.at[0], recv_sem=vol_recv.at[0],
                device_id=in_plane(d), device_id_type=MESH).start()
            return 0

        def send_b(d, _):
            pltpu.make_async_remote_copy(
                src_ref=part_b, dst_ref=slots_b.at[line], send_sem=vol_send.at[1], recv_sem=vol_recv.at[1],
                device_id=in_line(d), device_id_type=MESH).start()
            return 0

        all_a = wait_for_copies(slots_a, n_plane - 1, vol_send.at[0], vol_recv.at[0], in_plane(1))
        all_b = wait_for_copies(slots_b, n_line - 1, vol_send.at[1], vol_recv.at[1], in_line(1))

    def turn(x):
        for d in range(0, 192, 16):
            turned[x, :, d : d + 16] = jnp.swapaxes(adj[d : d + 16, x], 0, 1)

    def sense(x):
        inner = jnp.zeros((16, 128), F32)
        for c in range(0, 192, 16):
            inner = inner + jnp.sum(adj[c : c + 16, x].astype(F32) * vel[c : c + 16, x].astype(F32), axis=0)
        rho, scale = den[x], met[x]
        slope = -4.0 / ((1.0 + rho) * (1.0 + rho))
        live = jnp.where(ids[x] > 0, 1.0, 0.0)
        value = (live * slope * scale * inner * SENS_SCALE).astype(BF16).astype(F32)
        sens[x] = value
        send_lo[pl.ds(x, 1)] = value[0:1]
        send_hi[pl.ds(x, 1)] = value[15:16]

    def traces(x):
        rho, scale = den[x], met[x]
        alpha = 2.0 * (1.0 - rho) / (1.0 + rho)
        for y0 in range(0, 16, CHUNK):
            cols = jnp.concatenate([turned[x, y0 + j] for j in range(CHUNK)], axis=1)
            got = jnp.dot(weights[...], cols, preferred_element_type=F32)
            for j in range(CHUNK):
                y = y0 + j
                own = turned[x, y].astype(F32)
                total = got[0:192, j * 128 : (j + 1) * 128]
                base[x, y] = scale[y : y + 1] * (total + alpha[y : y + 1] * own)
            t = got[192:480]
            lanes = slice(y0 * 128, (y0 + CHUNK) * 128)
            later = slice(y0 * 128 + 128, (y0 + CHUNK) * 128 + 128)
            tx0[x + 1, :, lanes] = t[0:48].astype(BF16)
            tx1[x, :, lanes] = t[48:96].astype(BF16)
            ty2[x, :, later] = t[96:144].astype(BF16)
            ty3[x, :, lanes] = t[144:192].astype(BF16)
            for j in range(CHUNK):
                at = slice((y0 + j) * 128, (y0 + j + 1) * 128)
                tz4[x, :, at] = shift_lanes(t[192:240, j * 128 : (j + 1) * 128], False).astype(BF16)
                tz5[x, :, at] = shift_lanes(t[240:288, j * 128 : (j + 1) * 128], True).astype(BF16)

    def order(i):
        return lax.rem(i * (cx - 1), cx)

    def slab(i, _):
        x, ahead = order(i), order(i + 1)

        @pl.when(i < cx - 1)
        def _():
            adj_copy(ahead).wait()

        vel_copy(x).wait()
        traces(x)
        sense(x)
        turn(ahead)
        if remote:
            @pl.when(i == 0)
            def _():
                pl.semaphore_wait(barrier, n_plane + n_line)
                lax.fori_loop(1, n_plane, send_a, 0)
                x_down.start()

            @pl.when(i == 1)
            def _():
                x_up.start()

        return 0

    for c in small[:5]:
        c.wait()
    weights[0:192, :] = vol[...].T

    weighted = den[...] * met[...]
    lane = lax.broadcasted_iota(jnp.int32, (1, 128), 1)
    row = jnp.zeros((1, 128), F32)
    for g in range(GROUPS):
        mine = jnp.sum(jnp.where(ids[...] == g + 1, weighted, 0.0), axis=0)
        mine = jnp.sum(jnp.sum(mine, axis=0, keepdims=True), axis=1, keepdims=True)
        row = row + jnp.where(lane == g, mine, 0.0)
    part_a[...] = row
    if remote:
        slots_a[spot] = row

    adj_copy(0).wait()
    turn(0)
    lax.fori_loop(0, cx, slab, 0)
    if remote:
        @pl.when(span > 0)
        def _():
            y_down.start()
            q_down.start()

        @pl.when(span < n_span - 1)
        def _():
            y_up.start()
            q_up.start()

        s_down.start()
        s_up.start()

    small[6].wait()
    lift_weights[...] = lift[...].T
    small[5].wait()
    sign[...] = 1.0 - 2.0 * orient[...].astype(F32)

    if remote:
        all_a.wait_recv()
        total = slots_a[0]
        for s in range(1, n_plane):
            total = total + slots_a[s]
        part_b[...] = total
        slots_b[line] = total
        lax.fori_loop(1, n_line, send_b, 0)

    @pl.when(span == 0)
    def _():
        for x in range(cx):
            ty2[x, :, 0:128] = jnp.zeros((ROWS, 128), BF16)
        sy_lo[...] = jnp.zeros_like(sy_lo)

    @pl.when(span == n_span - 1)
    def _():
        for x in range(cx):
            ty3[x, :, 2048:2176] = jnp.zeros((ROWS, 128), BF16)
        sy_hi[...] = jnp.zeros_like(sy_hi)

    if remote:
        @pl.when(span > 0)
        def _():
            y_up.wait_recv()

        @pl.when(span < n_span - 1)
        def _():
            y_down.wait_recv()

    def lifted(x):
        for y0 in range(0, 16, CHUNK):
            lanes = slice(y0 * 128, (y0 + CHUNK) * 128)
            later = slice(y0 * 128 + 128, (y0 + CHUNK) * 128 + 128)
            faces = (tx0[x, :, lanes], tx1[x + 1, :, lanes], ty2[x, :, lanes], ty3[x, :, later], tz4[x, :, lanes], tz5[x, :, lanes])
            parts = []
            for k in range(6):
                rows = [jnp.broadcast_to(sign[k, x, y0 + j : y0 + j + 1], (ROWS, 128)) for j in range(CHUNK)]
                parts.append(faces[k] * jnp.concatenate(rows, axis=1).astype(BF16))
            got = jnp.dot(lift_weights[...], jnp.concatenate(parts, axis=0), preferred_element_type=F32)
            for j in range(CHUNK):
                back[x, y0 + j] = (base[x, y0 + j] + got[:, j * 128 : (j + 1) * 128]).astype(BF16)

    def turn_back(x):
        for d in range(0, 192, 16):
            held[d : d + 16, x] = jnp.swapaxes(back[x, :, d : d + 16], 0, 1)

    def late(i):
        return jnp.where(i < 2, i + 1, (cx - 1) * (i - 2))

    def finish(i, _):
        if remote:
            @pl.when(i == 2)
            def _():
                x_down.wait_recv()
                x_up.wait_recv()

        x = late(i)
        before = late(jnp.maximum(i - 1, 0))
        lifted(x)
        turn_back(before)
        return 0

    lax.fori_loop(0, cx, finish, 0)
    turn_back(late(cx - 1))

    if remote:
        @pl.when(span > 0)
        def _():
            y_down.wait_send()
            q_down.wait_send()
            q_up.wait_recv()

        @pl.when(span < n_span - 1)
        def _():
            y_up.wait_send()
            q_up.wait_send()
            q_down.wait_recv()

        s_down.wait()
        s_up.wait()
        x_down.wait_send()
        x_up.wait_send()
    else:
        for r in (sx_lo, sx_hi, sy_lo, sy_hi):
            r[...] = jnp.zeros_like(r)

    for x in range(cx):
        own = sens[x]
        below_x = sx_lo[...] if x == 0 else sens[x - 1]
        above_x = sx_hi[...] if x == cx - 1 else sens[x + 1]
        beside = below_x + above_x
        beside = beside + shift_rows(own, sy_lo[x : x + 1], False) + shift_rows(own, sy_hi[x : x + 1], True)
        beside = beside + shift_lanes(own, False) + shift_lanes(own, True)
        filt[x] = (own + FILTER_BETA * beside) / (1.0 + 6.0 * FILTER_BETA)

    if remote:
        all_b.wait_recv()
        volumes = slots_b[0]
        for s in range(1, n_line):
            volumes = volumes + slots_b[s]
        vol_out[...] = volumes * (1.0 / (den.shape[0] * den.shape[1] * den.shape[2]))
        all_a.wait_send()
        all_b.wait_send()
    else:
        vol_out[...] = part_a[...]


def second_kernel(held, filt_in, vol_in, res_hbm, filt, vol_out, out_sem):
    pieces = out_sem.shape[0]
    step = held.shape[0] // pieces
    copies = [
        pltpu.make_async_copy(held.at[pl.ds(i * step, step)], res_hbm.at[pl.ds(i * step, step)], out_sem.at[i])
        for i in range(pieces)
    ]
    for c in copies:
        c.start()
    filt[...] = filt_in[...]
    for g in range(GROUPS):
        vol_out[g] = vol_in[0, g]
    for c in copies:
        c.wait()


def in_hbm(array):
    return pltpu.with_memory_space_constraint(array, pltpu.HBM)


def shards(
    n_stream, n_span, remote,
    adjoint, velocity, density, metric, orientation, design_ids, volume_block, face_trace, face_lift
):
    cx = adjoint.shape[1]
    hbm_spec = pl.BlockSpec(memory_space=pltpu.HBM)
    vmem_spec = pl.BlockSpec(memory_space=pltpu.VMEM)
    dma = pltpu.SemaphoreType.DMA
    lift_rows = jnp.swapaxes(face_lift, 1, 2).reshape(288, 192)
    whole = (adjoint, velocity, density, metric, design_ids, orientation, volume_block, face_trace.reshape(288, 192), lift_rows)
    cells = (cx, 16, 128)
    dofs = (192, cx, 16, 128)
    mids = [(dofs, BF16), (cells, F32), ((1, 128), F32)]
    n_plane, n_line = PLANE * n_span, n_stream // PLANE
    mid = pl.pallas_call(
        functools.partial(first_kernel, n_stream, n_span, remote),
        out_shape=[pltpu.VMEM(s, d) for s, d in mids],
        in_specs=[hbm_spec] * len(whole),
        out_specs=[vmem_spec] * len(mids),
        scratch_shapes=[
            pltpu.VMEM(dofs, BF16),
            pltpu.VMEM(dofs, BF16),
            pltpu.VMEM(cells, F32),
            pltpu.VMEM(cells, F32),
            pltpu.VMEM(cells, jnp.int32),
            pltpu.VMEM((6, *cells), jnp.int32),
            pltpu.VMEM((192, 192), BF16),
            pltpu.VMEM((288, 192), BF16),
            pltpu.VMEM((480, 192), BF16),
            pltpu.VMEM((192, 288), BF16),
            pltpu.VMEM((6, *cells), F32),
            pltpu.VMEM((cx, 16, 192, 128), BF16),
            pltpu.VMEM((cx, 16, 192, 128), BF16),
            pltpu.VMEM((cx, 16, 192, 128), F32),
            pltpu.VMEM((cx + 1, ROWS, 2048), BF16),
            pltpu.VMEM((cx + 1, ROWS, 2048), BF16),
            pltpu.VMEM((cx, ROWS, 2176), BF16),
            pltpu.VMEM((cx, ROWS, 2176), BF16),
            pltpu.VMEM((cx, ROWS, 2048), BF16),
            pltpu.VMEM((cx, ROWS, 2048), BF16),
            pltpu.VMEM(cells, F32),
            pltpu.VMEM((16, 128), F32),
            pltpu.VMEM((16, 128), F32),
            pltpu.VMEM((8, 128), F32),
            pltpu.VMEM((8, 128), F32),
            pltpu.VMEM((8, 128), F32),
            pltpu.VMEM((8, 128), F32),
            pltpu.VMEM((n_plane, 1, 128), F32),
            pltpu.VMEM((max(n_line, 1), 1, 128), F32),
            pltpu.VMEM((1, 128), F32),
            pltpu.VMEM((1, 128), F32),
            dma((cx,)), dma((cx,)), dma((7,)), dma((8,)), dma((8,)), dma((2,)), dma((2,)),
        ],
        compiler_params=pltpu.CompilerParams(
            collective_id=0 if remote else None, has_side_effects=True, vmem_limit_bytes=44 * 2**20
        ),
    )(*[in_hbm(a) for a in whole])
    return pl.pallas_call(
        second_kernel,
        out_shape=[
            jax.ShapeDtypeStruct(adjoint.shape, BF16),
            jax.ShapeDtypeStruct(cells, F32),
            jax.ShapeDtypeStruct((GROUPS,), F32),
        ],
        in_specs=[vmem_spec] * len(mids),
        out_specs=[hbm_spec, vmem_spec, pl.BlockSpec(memory_space=pltpu.SMEM)],
        scratch_shapes=[dma((8,))],
        compiler_params=pltpu.CompilerParams(vmem_limit_bytes=4 * 2**20),
    )(*[pltpu.with_memory_space_constraint(m, pltpu.VMEM) for m in mid])


def solution(mesh, remote=True):
    cells = P("stream", "span", None)
    dofs = P(None, "stream", "span", None)
    return jax.shard_map(
        functools.partial(shards, mesh.shape["stream"], mesh.shape["span"], remote),
        mesh=mesh,
        in_specs=(dofs, dofs, cells, cells, dofs, cells, P(), P(), P()),
        out_specs=(dofs, cells, P()),
        check_vma=False,
    )
```

```python
import functools

import jax
import jax.numpy as jnp
from jax import lax
from jax.experimental import pallas as pl
from jax.experimental.pallas import tpu as pltpu
from jax.sharding import PartitionSpec as P

MESH = pl.DeviceIdType.MESH
F32 = jnp.float32
BF16 = jnp.bfloat16
GROUPS = 4
SENS_SCALE = 0.03125
FILTER_BETA = 0.5
ROWS = 48
CHUNK = 4
PLANE = 4


def shift_rows(field, first, up):
    row = lax.broadcasted_iota(jnp.int32, field.shape, 0)
    edge = field.shape[0] - 1 if up else 0
    moved = pltpu.roll(field, field.shape[0] - 1 if up else 1, 0)
    return jnp.where(row == edge, first, moved)


def shift_lanes(field, up):
    lane = lax.broadcasted_iota(jnp.int32, field.shape, field.ndim - 1)
    edge = 127 if up else 0
    moved = pltpu.roll(field, 127 if up else 1, field.ndim - 1)
    return jnp.where(lane == edge, jnp.zeros_like(field), moved)


def wait_for_copies(slots, count, send_sem, recv_sem, device):
    return pltpu.make_async_remote_copy(
        src_ref=slots.at[pl.ds(0, count)], dst_ref=slots.at[pl.ds(0, count)],
        send_sem=send_sem, recv_sem=recv_sem, device_id=device, device_id_type=MESH)


def first_kernel(
    n_stream, n_span, remote,
    adj_hbm, vel_hbm, den_hbm, met_hbm, ids_hbm, orient_hbm, vol_hbm, trace_hbm, lift_hbm,
    held, filt, vol_out,
    adj, vel, den, met, ids, orient, vol, lift, weights, lift_weights, sign, turned_a, turned_b, turned_c, turned_d, back_a, back_b, base,
    tx0, tx1, ty2, ty3, tz4, tz5, sens, sx_lo, sx_hi, sy_lo, sy_hi,
    send_lo, send_hi, slots_a, slots_b, part_a, part_b,
    in_sem, vel_sem, small_sem, halo_send, halo_recv, vol_send, vol_recv,
):
    cx = adj.shape[1]
    turned = (turned_a, turned_b, turned_c, turned_d)
    stream, span = lax.axis_index("stream"), lax.axis_index("span")
    left, right = lax.rem(stream + n_stream - 1, n_stream), lax.rem(stream + 1, n_stream)
    below, above = jnp.maximum(span - 1, 0), jnp.minimum(span + 1, n_span - 1)
    n_plane = PLANE * n_span
    n_line = n_stream // PLANE
    line, seat = stream // PLANE, lax.rem(stream, PLANE)
    spot = seat * n_span + span
    seats = [line * PLANE + lax.rem(seat + d, PLANE) for d in range(PLANE)]
    spans = [lax.rem(span + d, n_span) for d in range(n_span)]
    in_plane = [(seats[d // n_span], spans[d % n_span]) for d in range(n_plane - 1, 0, -1)]
    in_line = [(lax.rem(line + d, n_line) * PLANE + seat, span) for d in range(1, n_line)]

    def adj_copy(x):
        return pltpu.make_async_copy(adj_hbm.at[:, x], adj.at[:, x], in_sem.at[x])

    def vel_copy(x):
        return pltpu.make_async_copy(vel_hbm.at[:, x], vel.at[:, x], vel_sem.at[x])

    small = [
        pltpu.make_async_copy(a, b, small_sem.at[i])
        for i, (a, b) in enumerate((
            (vol_hbm, vol), (trace_hbm, weights.at[pl.ds(192, 288)]), (den_hbm, den), (met_hbm, met),
            (ids_hbm, ids), (orient_hbm, orient), (lift_hbm, lift)))
    ]
    vol_copy, trace_copy, den_copy, met_copy, ids_copy, orient_copy, lift_copy = small
    trace_copy.start()
    adj_copy(0).start()
    for c in (den_copy, met_copy, ids_copy):
        c.start()
    for x in (cx - 1, 2, 1):
        adj_copy(x).start()
    vol_copy.start()

    if remote:
        barrier = pltpu.get_barrier_semaphore()

        def greet(device):
            pl.semaphore_signal(barrier, inc=1, device_id=device, device_id_type=MESH)

        greet((left, span))
        greet((right, span))
        for device in in_plane + in_line:
            greet(device)

        def halo(i, src, dst, device):
            return pltpu.make_async_remote_copy(
                src_ref=src, dst_ref=dst, send_sem=halo_send.at[i], recv_sem=halo_recv.at[i],
                device_id=device, device_id_type=MESH)

        x_down = halo(0, tx1.at[0], tx1.at[cx], (left, span))
        x_up = halo(1, tx0.at[cx], tx0.at[0], (right, span))
        y_down = halo(2, ty3.at[:, :, pl.ds(0, 128)], ty3.at[:, :, pl.ds(2048, 128)], (stream, below))
        y_up = halo(3, ty2.at[:, :, pl.ds(2048, 128)], ty2.at[:, :, pl.ds(0, 128)], (stream, above))
        s_down = halo(4, sens.at[0], sx_hi, (left, span))
        s_up = halo(5, sens.at[cx - 1], sx_lo, (right, span))
        q_down = halo(6, send_lo, sy_hi, (stream, below))
        q_up = halo(7, send_hi, sy_lo, (stream, above))

        def send_to_all(devices, part, slot, i):
            for device in devices:
                pltpu.make_async_remote_copy(
                    src_ref=part, dst_ref=slot, send_sem=vol_send.at[i], recv_sem=vol_recv.at[i],
                    device_id=device, device_id_type=MESH).start()

        all_a = wait_for_copies(slots_a, n_plane - 1, vol_send.at[0], vol_recv.at[0], in_plane[0])
        all_b = wait_for_copies(slots_b, n_line - 1, vol_send.at[1], vol_recv.at[1], in_line[0])

    def turn(x, to):
        for d in range(0, 192, 16):
            to[:, d : d + 16] = jnp.swapaxes(adj[d : d + 16, x], 0, 1)

    def sense(x):
        inner = jnp.zeros((16, 128), F32)
        for c in range(0, 192, 16):
            inner = inner + jnp.sum(adj[c : c + 16, x].astype(F32) * vel[c : c + 16, x].astype(F32), axis=0)
        rho, scale = den[x], met[x]
        slope = -4.0 / ((1.0 + rho) * (1.0 + rho))
        live = jnp.where(ids[x] > 0, 1.0, 0.0)
        value = (live * slope * scale * inner * SENS_SCALE).astype(BF16).astype(F32)
        sens[x] = value
        send_lo[pl.ds(x, 1)] = value[0:1]
        send_hi[pl.ds(x, 1)] = value[15:16]

    def traces(x, turned):
        rho, scale = den[x], met[x]
        alpha = 2.0 * (1.0 - rho) / (1.0 + rho)
        for y0 in range(0, 16, CHUNK):
            cols = jnp.concatenate([turned[y0 + j] for j in range(CHUNK)], axis=1)
            got = jnp.dot(weights[...], cols, preferred_element_type=F32)
            for j in range(CHUNK):
                y = y0 + j
                own = turned[y].astype(F32)
                total = got[0:192, j * 128 : (j + 1) * 128]
                base[x, y] = scale[y : y + 1] * (total + alpha[y : y + 1] * own)
            t = got[192:480]
            lanes = slice(y0 * 128, (y0 + CHUNK) * 128)
            if x < cx - 1:
                tx0[x + 1, :, lanes] = t[0:48].astype(BF16)
            if x > 0:
                tx1[x, :, lanes] = t[48:96].astype(BF16)
            top = min(y0 + CHUNK, 15) - y0
            ty2[x, :, y0 * 128 + 128 : (y0 + top) * 128 + 128] = t[96:144, : top * 128].astype(BF16)
            low = max(y0, 1)
            ty3[x, :, low * 128 : (y0 + CHUNK) * 128] = t[144:192, (low - y0) * 128 :].astype(BF16)
            for j in range(CHUNK):
                at = slice((y0 + j) * 128, (y0 + j + 1) * 128)
                tz4[x, :, at] = shift_lanes(t[192:240, j * 128 : (j + 1) * 128], False).astype(BF16)
                tz5[x, :, at] = shift_lanes(t[240:288, j * 128 : (j + 1) * 128], True).astype(BF16)

    def face(k):
        return slice(192 + ROWS * k, 192 + ROWS * (k + 1))

    def edge_x(k, turned, to):
        for y0 in range(0, 16, CHUNK):
            cols = jnp.concatenate([turned[y0 + j] for j in range(CHUNK)], axis=1)
            got = jnp.dot(weights[face(k)], cols, preferred_element_type=F32)
            to[:, y0 * 128 : (y0 + CHUNK) * 128] = got.astype(BF16)

    def edge_y(k, y, to, at):
        cols = jnp.concatenate([t[y] for t in turned], axis=1)
        got = jnp.dot(weights[face(k)], cols, preferred_element_type=F32).astype(BF16)
        for x in range(cx):
            to[x, :, at : at + 128] = got[:, x * 128 : (x + 1) * 128]

    def service():
        if remote:
            all_a.wait_recv()
            total = slots_a[0]
            for s in range(1, n_plane):
                total = total + slots_a[s]
            part_b[...] = total
            slots_b[line] = total
            send_to_all(in_line, part_b, slots_b.at[line], 1)

    trace_copy.wait()
    adj_copy(0).wait()
    turn(0, turned[0])
    edge_x(1, turned[0], tx1.at[0])
    adj_copy(cx - 1).wait()
    turn(cx - 1, turned[cx - 1])
    edge_x(0, turned[cx - 1], tx0.at[cx])
    for c in (den_copy, met_copy, ids_copy):
        c.wait()

    weighted = den[...] * met[...]
    lane = lax.broadcasted_iota(jnp.int32, (1, 128), 1)
    row = jnp.zeros((1, 128), F32)
    for g in range(GROUPS):
        mine = jnp.sum(jnp.where(ids[...] == g + 1, weighted, 0.0), axis=0)
        mine = jnp.sum(jnp.sum(mine, axis=0, keepdims=True), axis=1, keepdims=True)
        row = row + jnp.where(lane == g, mine, 0.0)
    part_a[...] = row
    if remote:
        slots_a[spot] = row

    if remote:
        pl.semaphore_wait(barrier, n_plane + n_line)
        send_to_all(in_plane, part_a, slots_a.at[spot], 0)
        x_down.start()
        x_up.start()
    for x in (0, cx - 1, 2, 1):
        vel_copy(x).start()
    orient_copy.start()
    lift_copy.start()
    for x in (2, 1):
        adj_copy(x).wait()
        turn(x, turned[x])
    edge_y(3, 0, ty3, 0)
    edge_y(2, 15, ty2, 2048)
    if remote:
        @pl.when(span > 0)
        def _():
            y_down.start()

        @pl.when(span < n_span - 1)
        def _():
            y_up.start()

    vol_copy.wait()
    weights[0:192, :] = vol[...].T
    traces(0, turned[0])
    traces(cx - 1, turned[cx - 1])
    vel_copy(0).wait()
    vel_copy(cx - 1).wait()
    traces(2, turned[2])
    sense(0)
    sense(cx - 1)
    vel_copy(2).wait()
    vel_copy(1).wait()
    traces(1, turned[1])
    sense(2)
    sense(1)
    lift_copy.wait()
    lift_weights[...] = lift[...].T
    orient_copy.wait()
    sign[...] = 1.0 - 2.0 * orient[...].astype(F32)
    service()
    if remote:
        s_down.start()
        s_up.start()

        @pl.when(span > 0)
        def _():
            q_down.start()

        @pl.when(span < n_span - 1)
        def _():
            q_up.start()

    @pl.when(span == 0)
    def _():
        for x in range(cx):
            ty2[x, :, 0:128] = jnp.zeros((ROWS, 128), BF16)
        sy_lo[...] = jnp.zeros_like(sy_lo)

    @pl.when(span == n_span - 1)
    def _():
        for x in range(cx):
            ty3[x, :, 2048:2176] = jnp.zeros((ROWS, 128), BF16)
        sy_hi[...] = jnp.zeros_like(sy_hi)

    if remote:
        @pl.when(span > 0)
        def _():
            y_up.wait_recv()

        @pl.when(span < n_span - 1)
        def _():
            y_down.wait_recv()

    def lifted(x, back):
        for y0 in range(0, 16, CHUNK):
            lanes = slice(y0 * 128, (y0 + CHUNK) * 128)
            later = slice(y0 * 128 + 128, (y0 + CHUNK) * 128 + 128)
            faces = (tx0[x, :, lanes], tx1[x + 1, :, lanes], ty2[x, :, lanes], ty3[x, :, later], tz4[x, :, lanes], tz5[x, :, lanes])
            parts = []
            for k in range(6):
                rows = [jnp.broadcast_to(sign[k, x, y0 + j : y0 + j + 1], (ROWS, 128)) for j in range(CHUNK)]
                parts.append(faces[k] * jnp.concatenate(rows, axis=1).astype(BF16))
            got = jnp.dot(lift_weights[...], jnp.concatenate(parts, axis=0), preferred_element_type=F32)
            for j in range(CHUNK):
                back[y0 + j] = (base[x, y0 + j] + got[:, j * 128 : (j + 1) * 128]).astype(BF16)

    def turn_back(x, back):
        for d in range(0, 192, 16):
            held[d : d + 16, x] = jnp.swapaxes(back[:, d : d + 16], 0, 1)

    lifted(1, back_a)
    lifted(2, back_b)
    turn_back(1, back_a)
    if remote:
        x_up.wait_recv()
    lifted(0, back_a)
    turn_back(2, back_b)
    if remote:
        x_down.wait_recv()
    lifted(cx - 1, back_b)
    turn_back(0, back_a)
    turn_back(cx - 1, back_b)

    if remote:
        @pl.when(span > 0)
        def _():
            y_down.wait_send()
            q_down.wait_send()
            q_up.wait_recv()

        @pl.when(span < n_span - 1)
        def _():
            y_up.wait_send()
            q_up.wait_send()
            q_down.wait_recv()

        s_down.wait()
        s_up.wait()
        x_down.wait_send()
        x_up.wait_send()
    else:
        for r in (sx_lo, sx_hi, sy_lo, sy_hi):
            r[...] = jnp.zeros_like(r)

    for x in range(cx):
        own = sens[x]
        below_x = sx_lo[...] if x == 0 else sens[x - 1]
        above_x = sx_hi[...] if x == cx - 1 else sens[x + 1]
        beside = below_x + above_x
        beside = beside + shift_rows(own, sy_lo[x : x + 1], False) + shift_rows(own, sy_hi[x : x + 1], True)
        beside = beside + shift_lanes(own, False) + shift_lanes(own, True)
        filt[x] = (own + FILTER_BETA * beside) / (1.0 + 6.0 * FILTER_BETA)

    if remote:
        all_b.wait_recv()
        volumes = slots_b[0]
        for s in range(1, n_line):
            volumes = volumes + slots_b[s]
        vol_out[...] = volumes * (1.0 / (den.shape[0] * den.shape[1] * den.shape[2]))
        all_a.wait_send()
        all_b.wait_send()
    else:
        vol_out[...] = part_a[...]


def second_kernel(held, filt_in, vol_in, res_hbm, filt, vol_out, out_sem):
    pieces = out_sem.shape[0]
    step = held.shape[0] // pieces
    copies = [
        pltpu.make_async_copy(held.at[pl.ds(i * step, step)], res_hbm.at[pl.ds(i * step, step)], out_sem.at[i])
        for i in range(pieces)
    ]
    for c in copies:
        c.start()
    filt[...] = filt_in[...]
    for g in range(GROUPS):
        vol_out[g] = vol_in[0, g]
    for c in copies:
        c.wait()


def in_hbm(array):
    return pltpu.with_memory_space_constraint(array, pltpu.HBM)


def shards(
    n_stream, n_span, remote,
    adjoint, velocity, density, metric, orientation, design_ids, volume_block, face_trace, face_lift
):
    cx = adjoint.shape[1]
    hbm_spec = pl.BlockSpec(memory_space=pltpu.HBM)
    vmem_spec = pl.BlockSpec(memory_space=pltpu.VMEM)
    dma = pltpu.SemaphoreType.DMA
    lift_rows = jnp.swapaxes(face_lift, 1, 2).reshape(288, 192)
    whole = (adjoint, velocity, density, metric, design_ids, orientation, volume_block, face_trace.reshape(288, 192), lift_rows)
    cells = (cx, 16, 128)
    dofs = (192, cx, 16, 128)
    mids = [(dofs, BF16), (cells, F32), ((1, 128), F32)]
    n_plane, n_line = PLANE * n_span, n_stream // PLANE
    mid = pl.pallas_call(
        functools.partial(first_kernel, n_stream, n_span, remote),
        out_shape=[pltpu.VMEM(s, d) for s, d in mids],
        in_specs=[hbm_spec] * len(whole),
        out_specs=[vmem_spec] * len(mids),
        scratch_shapes=[
            pltpu.VMEM(dofs, BF16),
            pltpu.VMEM(dofs, BF16),
            pltpu.VMEM(cells, F32),
            pltpu.VMEM(cells, F32),
            pltpu.VMEM(cells, jnp.int32),
            pltpu.VMEM((6, *cells), jnp.int32),
            pltpu.VMEM((192, 192), BF16),
            pltpu.VMEM((288, 192), BF16),
            pltpu.VMEM((480, 192), BF16),
            pltpu.VMEM((192, 288), BF16),
            pltpu.VMEM((6, *cells), F32),
            *[pltpu.VMEM((16, 192, 128), BF16)] * 6,
            pltpu.VMEM((cx, 16, 192, 128), F32),
            pltpu.VMEM((cx + 1, ROWS, 2048), BF16),
            pltpu.VMEM((cx + 1, ROWS, 2048), BF16),
            pltpu.VMEM((cx, ROWS, 2176), BF16),
            pltpu.VMEM((cx, ROWS, 2176), BF16),
            pltpu.VMEM((cx, ROWS, 2048), BF16),
            pltpu.VMEM((cx, ROWS, 2048), BF16),
            pltpu.VMEM(cells, F32),
            pltpu.VMEM((16, 128), F32),
            pltpu.VMEM((16, 128), F32),
            pltpu.VMEM((8, 128), F32),
            pltpu.VMEM((8, 128), F32),
            pltpu.VMEM((8, 128), F32),
            pltpu.VMEM((8, 128), F32),
            pltpu.VMEM((n_plane, 1, 128), F32),
            pltpu.VMEM((max(n_line, 1), 1, 128), F32),
            pltpu.VMEM((1, 128), F32),
            pltpu.VMEM((1, 128), F32),
            dma((cx,)), dma((cx,)), dma((7,)), dma((8,)), dma((8,)), dma((2,)), dma((2,)),
        ],
        compiler_params=pltpu.CompilerParams(
            collective_id=0 if remote else None, has_side_effects=True, vmem_limit_bytes=44 * 2**20
        ),
    )(*[in_hbm(a) for a in whole])
    return pl.pallas_call(
        second_kernel,
        out_shape=[
            jax.ShapeDtypeStruct(adjoint.shape, BF16),
            jax.ShapeDtypeStruct(cells, F32),
            jax.ShapeDtypeStruct((GROUPS,), F32),
        ],
        in_specs=[vmem_spec] * len(mids),
        out_specs=[hbm_spec, vmem_spec, pl.BlockSpec(memory_space=pltpu.SMEM)],
        scratch_shapes=[dma((8,))],
        compiler_params=pltpu.CompilerParams(vmem_limit_bytes=4 * 2**20),
    )(*[pltpu.with_memory_space_constraint(m, pltpu.VMEM) for m in mid])


def solution(mesh, remote=True):
    cells = P("stream", "span", None)
    dofs = P(None, "stream", "span", None)
    return jax.shard_map(
        functools.partial(shards, mesh.shape["stream"], mesh.shape["span"], remote),
        mesh=mesh,
        in_specs=(dofs, dofs, cells, cells, dofs, cells, P(), P(), P()),
        out_specs=(dofs, cells, P()),
        check_vma=False,
    )
```

```python
import functools

import jax
import jax.numpy as jnp
from jax import lax
from jax.experimental import pallas as pl
from jax.experimental.pallas import tpu as pltpu
from jax.sharding import PartitionSpec as P

MESH = pl.DeviceIdType.MESH
F32 = jnp.float32
BF16 = jnp.bfloat16
GROUPS = 4
SENS_SCALE = 0.03125
FILTER_BETA = 0.5
ROWS = 48
CHUNK = 4
PLANE = 4


def shift_rows(field, first, up):
    row = lax.broadcasted_iota(jnp.int32, field.shape, 0)
    edge = field.shape[0] - 1 if up else 0
    moved = pltpu.roll(field, field.shape[0] - 1 if up else 1, 0)
    return jnp.where(row == edge, first, moved)


def shift_lanes(field, up):
    lane = lax.broadcasted_iota(jnp.int32, field.shape, field.ndim - 1)
    edge = 127 if up else 0
    moved = pltpu.roll(field, 127 if up else 1, field.ndim - 1)
    return jnp.where(lane == edge, jnp.zeros_like(field), moved)


def wait_for_copies(slots, count, send_sem, recv_sem, device):
    return pltpu.make_async_remote_copy(
        src_ref=slots.at[pl.ds(0, count)], dst_ref=slots.at[pl.ds(0, count)],
        send_sem=send_sem, recv_sem=recv_sem, device_id=device, device_id_type=MESH)


def first_kernel(
    n_stream, n_span, remote,
    adj_hbm, vel_hbm, den_hbm, met_hbm, ids_hbm, orient_hbm, vol_hbm, trace_hbm, lift_hbm,
    held, filt, vol_out,
    adj, vel, den, met, ids, orient, vol, lift, weights, lift_weights, sign, turned_a, turned_b, turned_c, turned_d, back_a, back_b, base,
    tx0, tx1, ty2, ty3, tz4, tz5, sens, sx_lo, sx_hi, sy_lo, sy_hi,
    send_lo, send_hi, slots_a, slots_b, part_a, part_b,
    in_sem, vel_sem, small_sem, halo_send, halo_recv, vol_send, vol_recv,
):
    cx = adj.shape[1]
    turned = (turned_a, turned_b, turned_c, turned_d)
    stream, span = lax.axis_index("stream"), lax.axis_index("span")
    left, right = lax.rem(stream + n_stream - 1, n_stream), lax.rem(stream + 1, n_stream)
    below, above = jnp.maximum(span - 1, 0), jnp.minimum(span + 1, n_span - 1)
    n_plane = PLANE * n_span
    n_line = n_stream // PLANE
    line, seat = stream // PLANE, lax.rem(stream, PLANE)
    spot = seat * n_span + span
    seats = [line * PLANE + lax.rem(seat + d, PLANE) for d in range(PLANE)]
    spans = [lax.rem(span + d, n_span) for d in range(n_span)]
    in_plane = [(seats[d // n_span], spans[d % n_span]) for d in range(n_plane - 1, 0, -1)]
    in_line = [(lax.rem(line + d, n_line) * PLANE + seat, span) for d in range(1, n_line)]

    def adj_copy(x):
        return pltpu.make_async_copy(adj_hbm.at[:, x], adj.at[:, x], in_sem.at[x])

    def vel_copy(x):
        return pltpu.make_async_copy(vel_hbm.at[:, x], vel.at[:, x], vel_sem.at[x])

    small = [
        pltpu.make_async_copy(a, b, small_sem.at[i])
        for i, (a, b) in enumerate((
            (vol_hbm, vol), (trace_hbm, weights.at[pl.ds(192, 288)]), (den_hbm, den), (met_hbm, met),
            (ids_hbm, ids), (orient_hbm, orient), (lift_hbm, lift)))
    ]
    vol_copy, trace_copy, den_copy, met_copy, ids_copy, orient_copy, lift_copy = small
    trace_copy.start()
    adj_copy(0).start()
    for c in (den_copy, met_copy, ids_copy):
        c.start()
    for x in (cx - 1, 2, 1):
        adj_copy(x).start()
    vol_copy.start()

    if remote:
        barrier = pltpu.get_barrier_semaphore()

        def greet(device):
            pl.semaphore_signal(barrier, inc=1, device_id=device, device_id_type=MESH)

        greet((left, span))
        greet((right, span))
        for device in in_plane + in_line:
            greet(device)

        def halo(i, src, dst, device):
            return pltpu.make_async_remote_copy(
                src_ref=src, dst_ref=dst, send_sem=halo_send.at[i], recv_sem=halo_recv.at[i],
                device_id=device, device_id_type=MESH)

        x_down = halo(0, tx1.at[0], tx1.at[cx], (left, span))
        x_up = halo(1, tx0.at[cx], tx0.at[0], (right, span))
        y_down = halo(2, ty3.at[:, :, pl.ds(0, 128)], ty3.at[:, :, pl.ds(2048, 128)], (stream, below))
        y_up = halo(3, ty2.at[:, :, pl.ds(2048, 128)], ty2.at[:, :, pl.ds(0, 128)], (stream, above))
        s_down = halo(4, sens.at[0], sx_hi, (left, span))
        s_up = halo(5, sens.at[cx - 1], sx_lo, (right, span))
        q_down = halo(6, send_lo, sy_hi, (stream, below))
        q_up = halo(7, send_hi, sy_lo, (stream, above))

        def send_to_all(devices, part, slot, i):
            for device in devices:
                pltpu.make_async_remote_copy(
                    src_ref=part, dst_ref=slot, send_sem=vol_send.at[i], recv_sem=vol_recv.at[i],
                    device_id=device, device_id_type=MESH).start()

        all_a = wait_for_copies(slots_a, n_plane - 1, vol_send.at[0], vol_recv.at[0], in_plane[0])
        all_b = wait_for_copies(slots_b, n_line - 1, vol_send.at[1], vol_recv.at[1], in_line[0])

    def turn(x, to):
        for d in range(0, 192, 16):
            to[:, d : d + 16] = jnp.swapaxes(adj[d : d + 16, x], 0, 1)

    def sense(x):
        inner = jnp.zeros((16, 128), F32)
        for c in range(0, 192, 16):
            inner = inner + jnp.sum(adj[c : c + 16, x].astype(F32) * vel[c : c + 16, x].astype(F32), axis=0)
        rho, scale = den[x], met[x]
        slope = -4.0 / ((1.0 + rho) * (1.0 + rho))
        live = jnp.where(ids[x] > 0, 1.0, 0.0)
        value = (live * slope * scale * inner * SENS_SCALE).astype(BF16).astype(F32)
        sens[x] = value
        send_lo[pl.ds(x, 1)] = value[0:1]
        send_hi[pl.ds(x, 1)] = value[15:16]

    def traces(x, turned):
        rho, scale = den[x], met[x]
        alpha = 2.0 * (1.0 - rho) / (1.0 + rho)
        for y0 in range(0, 16, CHUNK):
            cols = jnp.concatenate([turned[y0 + j] for j in range(CHUNK)], axis=1)
            got = jnp.dot(weights[...], cols, preferred_element_type=F32)
            for j in range(CHUNK):
                y = y0 + j
                own = turned[y].astype(F32)
                total = got[0:192, j * 128 : (j + 1) * 128]
                base[x, y] = scale[y : y + 1] * (total + alpha[y : y + 1] * own)
            t = got[192:480]
            lanes = slice(y0 * 128, (y0 + CHUNK) * 128)
            if x < cx - 1:
                tx0[x + 1, :, lanes] = t[0:48].astype(BF16)
            if x > 0:
                tx1[x, :, lanes] = t[48:96].astype(BF16)
            top = min(y0 + CHUNK, 15) - y0
            ty2[x, :, y0 * 128 + 128 : (y0 + top) * 128 + 128] = t[96:144, : top * 128].astype(BF16)
            low = max(y0, 1)
            ty3[x, :, low * 128 : (y0 + CHUNK) * 128] = t[144:192, (low - y0) * 128 :].astype(BF16)
            for j in range(CHUNK):
                at = slice((y0 + j) * 128, (y0 + j + 1) * 128)
                tz4[x, :, at] = shift_lanes(t[192:240, j * 128 : (j + 1) * 128], False).astype(BF16)
                tz5[x, :, at] = shift_lanes(t[240:288, j * 128 : (j + 1) * 128], True).astype(BF16)

    def face(k):
        return slice(192 + ROWS * k, 192 + ROWS * (k + 1))

    def edge_x(k, turned, to):
        for y0 in range(0, 16, CHUNK):
            cols = jnp.concatenate([turned[y0 + j] for j in range(CHUNK)], axis=1)
            got = jnp.dot(weights[face(k)], cols, preferred_element_type=F32)
            to[:, y0 * 128 : (y0 + CHUNK) * 128] = got.astype(BF16)

    def edge_y(k, y, to, at):
        cols = jnp.concatenate([t[y] for t in turned], axis=1)
        got = jnp.dot(weights[face(k)], cols, preferred_element_type=F32).astype(BF16)
        for x in range(cx):
            to[x, :, at : at + 128] = got[:, x * 128 : (x + 1) * 128]

    def service():
        if remote:
            all_a.wait_recv()
            total = slots_a[0]
            for s in range(1, n_plane):
                total = total + slots_a[s]
            part_b[...] = total
            slots_b[line] = total
            send_to_all(in_line, part_b, slots_b.at[line], 1)

    trace_copy.wait()
    adj_copy(0).wait()
    turn(0, turned[0])
    edge_x(1, turned[0], tx1.at[0])
    adj_copy(cx - 1).wait()
    turn(cx - 1, turned[cx - 1])
    edge_x(0, turned[cx - 1], tx0.at[cx])
    for c in (den_copy, met_copy, ids_copy):
        c.wait()

    weighted = den[...] * met[...]
    lane = lax.broadcasted_iota(jnp.int32, (1, 128), 1)
    row = jnp.zeros((1, 128), F32)
    for g in range(GROUPS):
        mine = jnp.sum(jnp.where(ids[...] == g + 1, weighted, 0.0), axis=0)
        mine = jnp.sum(jnp.sum(mine, axis=0, keepdims=True), axis=1, keepdims=True)
        row = row + jnp.where(lane == g, mine, 0.0)
    part_a[...] = row
    if remote:
        slots_a[spot] = row

    if remote:
        pl.semaphore_wait(barrier, n_plane + n_line)
        send_to_all(in_plane, part_a, slots_a.at[spot], 0)
        x_down.start()
        x_up.start()
    for x in (0, cx - 1, 2, 1):
        vel_copy(x).start()
    orient_copy.start()
    lift_copy.start()
    for x in (2, 1):
        adj_copy(x).wait()
        turn(x, turned[x])
    edge_y(3, 0, ty3, 0)
    edge_y(2, 15, ty2, 2048)
    if remote:
        @pl.when(span > 0)
        def _():
            y_down.start()

        @pl.when(span < n_span - 1)
        def _():
            y_up.start()

    vol_copy.wait()
    weights[0:192, :] = vol[...].T
    traces(0, turned[0])
    traces(cx - 1, turned[cx - 1])
    vel_copy(0).wait()
    vel_copy(cx - 1).wait()
    traces(2, turned[2])
    sense(0)
    sense(cx - 1)
    vel_copy(2).wait()
    vel_copy(1).wait()
    traces(1, turned[1])
    sense(2)
    sense(1)
    lift_copy.wait()
    lift_weights[...] = lift[...].T
    orient_copy.wait()
    sign[...] = 1.0 - 2.0 * orient[...].astype(F32)
    if remote:
        s_down.start()
        s_up.start()

        @pl.when(span > 0)
        def _():
            q_down.start()

        @pl.when(span < n_span - 1)
        def _():
            q_up.start()

    service()

    @pl.when(span == 0)
    def _():
        for x in range(cx):
            ty2[x, :, 0:128] = jnp.zeros((ROWS, 128), BF16)
        sy_lo[...] = jnp.zeros_like(sy_lo)

    @pl.when(span == n_span - 1)
    def _():
        for x in range(cx):
            ty3[x, :, 2048:2176] = jnp.zeros((ROWS, 128), BF16)
        sy_hi[...] = jnp.zeros_like(sy_hi)

    if remote:
        @pl.when(span > 0)
        def _():
            y_up.wait_recv()

        @pl.when(span < n_span - 1)
        def _():
            y_down.wait_recv()

    def lifted(x, back):
        for y0 in range(0, 16, CHUNK):
            lanes = slice(y0 * 128, (y0 + CHUNK) * 128)
            later = slice(y0 * 128 + 128, (y0 + CHUNK) * 128 + 128)
            faces = (tx0[x, :, lanes], tx1[x + 1, :, lanes], ty2[x, :, lanes], ty3[x, :, later], tz4[x, :, lanes], tz5[x, :, lanes])
            parts = []
            for k in range(6):
                rows = [jnp.broadcast_to(sign[k, x, y0 + j : y0 + j + 1], (ROWS, 128)) for j in range(CHUNK)]
                parts.append(faces[k] * jnp.concatenate(rows, axis=1).astype(BF16))
            got = jnp.dot(lift_weights[...], jnp.concatenate(parts, axis=0), preferred_element_type=F32)
            for j in range(CHUNK):
                back[y0 + j] = (base[x, y0 + j] + got[:, j * 128 : (j + 1) * 128]).astype(BF16)

    def turn_back(x, back):
        for d in range(0, 192, 16):
            held[d : d + 16, x] = jnp.swapaxes(back[:, d : d + 16], 0, 1)

    lifted(1, back_a)
    lifted(2, back_b)
    turn_back(1, back_a)
    core = lax.rem(stream, 2)
    soon = (1 - core) * (cx - 1)
    late = core * (cx - 1)
    if remote:
        @pl.when(core == 0)
        def _():
            x_down.wait_recv()

        @pl.when(core == 1)
        def _():
            x_up.wait_recv()

    lifted(soon, back_a)
    turn_back(2, back_b)
    turn_back(soon, back_a)
    if remote:
        @pl.when(core == 0)
        def _():
            x_up.wait_recv()

        @pl.when(core == 1)
        def _():
            x_down.wait_recv()

    lifted(late, back_b)
    turn_back(late, back_b)

    if remote:
        @pl.when(span > 0)
        def _():
            q_up.wait_recv()

        @pl.when(span < n_span - 1)
        def _():
            q_down.wait_recv()

        s_down.wait_recv()
        s_up.wait_recv()
    else:
        for r in (sx_lo, sx_hi, sy_lo, sy_hi):
            r[...] = jnp.zeros_like(r)

    for x in range(cx):
        own = sens[x]
        below_x = sx_lo[...] if x == 0 else sens[x - 1]
        above_x = sx_hi[...] if x == cx - 1 else sens[x + 1]
        beside = below_x + above_x
        beside = beside + shift_rows(own, sy_lo[x : x + 1], False) + shift_rows(own, sy_hi[x : x + 1], True)
        beside = beside + shift_lanes(own, False) + shift_lanes(own, True)
        filt[x] = (own + FILTER_BETA * beside) / (1.0 + 6.0 * FILTER_BETA)

    if remote:
        @pl.when(span > 0)
        def _():
            y_down.wait_send()
            q_down.wait_send()

        @pl.when(span < n_span - 1)
        def _():
            y_up.wait_send()
            q_up.wait_send()

        s_down.wait_send()
        s_up.wait_send()
        x_down.wait_send()
        x_up.wait_send()

    if remote:
        all_b.wait_recv()
        volumes = slots_b[0]
        for s in range(1, n_line):
            volumes = volumes + slots_b[s]
        vol_out[...] = volumes * (1.0 / (den.shape[0] * den.shape[1] * den.shape[2]))
        all_a.wait_send()
        all_b.wait_send()
    else:
        vol_out[...] = part_a[...]


def second_kernel(held, filt_in, vol_in, res_hbm, filt, vol_out, out_sem):
    pieces = out_sem.shape[0]
    step = held.shape[0] // pieces
    copies = [
        pltpu.make_async_copy(held.at[pl.ds(i * step, step)], res_hbm.at[pl.ds(i * step, step)], out_sem.at[i])
        for i in range(pieces)
    ]
    for c in copies:
        c.start()
    filt[...] = filt_in[...]
    for g in range(GROUPS):
        vol_out[g] = vol_in[0, g]
    for c in copies:
        c.wait()


def in_hbm(array):
    return pltpu.with_memory_space_constraint(array, pltpu.HBM)


def shards(
    n_stream, n_span, remote,
    adjoint, velocity, density, metric, orientation, design_ids, volume_block, face_trace, face_lift
):
    cx = adjoint.shape[1]
    hbm_spec = pl.BlockSpec(memory_space=pltpu.HBM)
    vmem_spec = pl.BlockSpec(memory_space=pltpu.VMEM)
    dma = pltpu.SemaphoreType.DMA
    lift_rows = jnp.swapaxes(face_lift, 1, 2).reshape(288, 192)
    whole = (adjoint, velocity, density, metric, design_ids, orientation, volume_block, face_trace.reshape(288, 192), lift_rows)
    cells = (cx, 16, 128)
    dofs = (192, cx, 16, 128)
    mids = [(dofs, BF16), (cells, F32), ((1, 128), F32)]
    n_plane, n_line = PLANE * n_span, n_stream // PLANE
    mid = pl.pallas_call(
        functools.partial(first_kernel, n_stream, n_span, remote),
        out_shape=[pltpu.VMEM(s, d) for s, d in mids],
        in_specs=[hbm_spec] * len(whole),
        out_specs=[vmem_spec] * len(mids),
        scratch_shapes=[
            pltpu.VMEM(dofs, BF16),
            pltpu.VMEM(dofs, BF16),
            pltpu.VMEM(cells, F32),
            pltpu.VMEM(cells, F32),
            pltpu.VMEM(cells, jnp.int32),
            pltpu.VMEM((6, *cells), jnp.int32),
            pltpu.VMEM((192, 192), BF16),
            pltpu.VMEM((288, 192), BF16),
            pltpu.VMEM((480, 192), BF16),
            pltpu.VMEM((192, 288), BF16),
            pltpu.VMEM((6, *cells), F32),
            *[pltpu.VMEM((16, 192, 128), BF16)] * 6,
            pltpu.VMEM((cx, 16, 192, 128), F32),
            pltpu.VMEM((cx + 1, ROWS, 2048), BF16),
            pltpu.VMEM((cx + 1, ROWS, 2048), BF16),
            pltpu.VMEM((cx, ROWS, 2176), BF16),
            pltpu.VMEM((cx, ROWS, 2176), BF16),
            pltpu.VMEM((cx, ROWS, 2048), BF16),
            pltpu.VMEM((cx, ROWS, 2048), BF16),
            pltpu.VMEM(cells, F32),
            pltpu.VMEM((16, 128), F32),
            pltpu.VMEM((16, 128), F32),
            pltpu.VMEM((8, 128), F32),
            pltpu.VMEM((8, 128), F32),
            pltpu.VMEM((8, 128), F32),
            pltpu.VMEM((8, 128), F32),
            pltpu.VMEM((n_plane, 1, 128), F32),
            pltpu.VMEM((max(n_line, 1), 1, 128), F32),
            pltpu.VMEM((1, 128), F32),
            pltpu.VMEM((1, 128), F32),
            dma((cx,)), dma((cx,)), dma((7,)), dma((8,)), dma((8,)), dma((2,)), dma((2,)),
        ],
        compiler_params=pltpu.CompilerParams(
            collective_id=0 if remote else None, has_side_effects=True, vmem_limit_bytes=44 * 2**20
        ),
    )(*[in_hbm(a) for a in whole])
    return pl.pallas_call(
        second_kernel,
        out_shape=[
            jax.ShapeDtypeStruct(adjoint.shape, BF16),
            jax.ShapeDtypeStruct(cells, F32),
            jax.ShapeDtypeStruct((GROUPS,), F32),
        ],
        in_specs=[vmem_spec] * len(mids),
        out_specs=[hbm_spec, vmem_spec, pl.BlockSpec(memory_space=pltpu.SMEM)],
        scratch_shapes=[dma((8,))],
        compiler_params=pltpu.CompilerParams(vmem_limit_bytes=4 * 2**20),
    )(*[pltpu.with_memory_space_constraint(m, pltpu.VMEM) for m in mid])


def solution(mesh, remote=True):
    cells = P("stream", "span", None)
    dofs = P(None, "stream", "span", None)
    return jax.shard_map(
        functools.partial(shards, mesh.shape["stream"], mesh.shape["span"], remote),
        mesh=mesh,
        in_specs=(dofs, dofs, cells, cells, dofs, cells, P(), P(), P()),
        out_specs=(dofs, cells, P()),
        check_vma=False,
    )
```

```python
import functools

import jax
import jax.numpy as jnp
from jax import lax
from jax.experimental import pallas as pl
from jax.experimental.pallas import tpu as pltpu
from jax.sharding import PartitionSpec as P

MESH = pl.DeviceIdType.MESH
F32 = jnp.float32
BF16 = jnp.bfloat16
GROUPS = 4
SENS_SCALE = 0.03125
FILTER_BETA = 0.5
ROWS = 48
CHUNK = 4
PLANE = 4


def shift_rows(field, first, up):
    row = lax.broadcasted_iota(jnp.int32, field.shape, 0)
    edge = field.shape[0] - 1 if up else 0
    moved = pltpu.roll(field, field.shape[0] - 1 if up else 1, 0)
    return jnp.where(row == edge, first, moved)


def shift_lanes(field, up):
    lane = lax.broadcasted_iota(jnp.int32, field.shape, field.ndim - 1)
    edge = 127 if up else 0
    moved = pltpu.roll(field, 127 if up else 1, field.ndim - 1)
    return jnp.where(lane == edge, jnp.zeros_like(field), moved)


def wait_for_copies(slots, count, send_sem, recv_sem, device):
    return pltpu.make_async_remote_copy(
        src_ref=slots.at[pl.ds(0, count)], dst_ref=slots.at[pl.ds(0, count)],
        send_sem=send_sem, recv_sem=recv_sem, device_id=device, device_id_type=MESH)


def first_kernel(
    n_stream, n_span, remote,
    adj_hbm, vel_hbm, den_hbm, met_hbm, ids_hbm, orient_hbm, vol_hbm, trace_hbm, lift_hbm,
    held, filt, vol_out,
    adj, vel, den, met, ids, orient, vol, lift, weights, lift_weights, sign, turned_a, turned_b, turned_c, turned_d, back_a, back_b, base,
    tx0, tx1, ty2, ty3, tz4, tz5, sens, sx_lo, sx_hi, sy_lo, sy_hi,
    send_lo, send_hi, slots_a, slots_b, part_a, part_b,
    in_sem, vel_sem, small_sem, halo_send, halo_recv, vol_send, vol_recv,
):
    cx = adj.shape[1]
    turned = (turned_a, turned_b, turned_c, turned_d)
    stream, span = lax.axis_index("stream"), lax.axis_index("span")
    left, right = lax.rem(stream + n_stream - 1, n_stream), lax.rem(stream + 1, n_stream)
    below, above = jnp.maximum(span - 1, 0), jnp.minimum(span + 1, n_span - 1)
    n_plane = PLANE * n_span
    n_line = n_stream // PLANE
    line, seat = stream // PLANE, lax.rem(stream, PLANE)
    spot = seat * n_span + span
    seats = [line * PLANE + lax.rem(seat + d, PLANE) for d in range(PLANE)]
    spans = [lax.rem(span + d, n_span) for d in range(n_span)]
    in_plane = [(seats[d // n_span], spans[d % n_span]) for d in range(n_plane - 1, 0, -1)]
    in_line = [(lax.rem(line + d, n_line) * PLANE + seat, span) for d in range(1, n_line)]

    def adj_copy(x):
        return pltpu.make_async_copy(adj_hbm.at[:, x], adj.at[:, x], in_sem.at[x])

    def vel_copy(x):
        return pltpu.make_async_copy(vel_hbm.at[:, x], vel.at[:, x], vel_sem.at[x])

    small = [
        pltpu.make_async_copy(a, b, small_sem.at[i])
        for i, (a, b) in enumerate((
            (vol_hbm, vol), (trace_hbm, weights.at[pl.ds(192, 288)]), (den_hbm, den), (met_hbm, met),
            (ids_hbm, ids), (orient_hbm, orient), (lift_hbm, lift)))
    ]
    vol_copy, trace_copy, den_copy, met_copy, ids_copy, orient_copy, lift_copy = small
    trace_copy.start()
    adj_copy(0).start()
    for c in (den_copy, met_copy, ids_copy):
        c.start()
    for x in (cx - 1, 2, 1):
        adj_copy(x).start()
    vol_copy.start()

    if remote:
        barrier = pltpu.get_barrier_semaphore()

        def greet(device):
            pl.semaphore_signal(barrier, inc=1, device_id=device, device_id_type=MESH)

        greet((left, span))
        greet((right, span))
        for device in in_plane + in_line:
            greet(device)

        def halo(i, src, dst, device):
            return pltpu.make_async_remote_copy(
                src_ref=src, dst_ref=dst, send_sem=halo_send.at[i], recv_sem=halo_recv.at[i],
                device_id=device, device_id_type=MESH)

        x_down = halo(0, tx1.at[0], tx1.at[cx], (left, span))
        x_up = halo(1, tx0.at[cx], tx0.at[0], (right, span))
        y_down = halo(2, ty3.at[:, :, pl.ds(0, 128)], ty3.at[:, :, pl.ds(2048, 128)], (stream, below))
        y_up = halo(3, ty2.at[:, :, pl.ds(2048, 128)], ty2.at[:, :, pl.ds(0, 128)], (stream, above))
        s_down = halo(4, sens.at[0], sx_hi, (left, span))
        s_up = halo(5, sens.at[cx - 1], sx_lo, (right, span))
        q_down = halo(6, send_lo, sy_hi, (stream, below))
        q_up = halo(7, send_hi, sy_lo, (stream, above))

        def send_to_all(devices, part, slot, i):
            for device in devices:
                pltpu.make_async_remote_copy(
                    src_ref=part, dst_ref=slot, send_sem=vol_send.at[i], recv_sem=vol_recv.at[i],
                    device_id=device, device_id_type=MESH).start()

        all_a = wait_for_copies(slots_a, n_plane - 1, vol_send.at[0], vol_recv.at[0], in_plane[0])
        all_b = wait_for_copies(slots_b, n_line - 1, vol_send.at[1], vol_recv.at[1], in_line[0])

    def turn(x, to):
        for d in range(0, 192, 16):
            to[:, d : d + 16] = jnp.swapaxes(adj[d : d + 16, x], 0, 1)

    def sense(x):
        inner = jnp.zeros((16, 128), F32)
        for c in range(0, 192, 16):
            inner = inner + jnp.sum(adj[c : c + 16, x].astype(F32) * vel[c : c + 16, x].astype(F32), axis=0)
        rho, scale = den[x], met[x]
        slope = -4.0 / ((1.0 + rho) * (1.0 + rho))
        live = jnp.where(ids[x] > 0, 1.0, 0.0)
        value = (live * slope * scale * inner * SENS_SCALE).astype(BF16).astype(F32)
        sens[x] = value
        send_lo[pl.ds(x, 1)] = value[0:1]
        send_hi[pl.ds(x, 1)] = value[15:16]

    def traces(x, turned):
        rho, scale = den[x], met[x]
        alpha = 2.0 * (1.0 - rho) / (1.0 + rho)
        for y0 in range(0, 16, CHUNK):
            cols = jnp.concatenate([turned[y0 + j] for j in range(CHUNK)], axis=1)
            got = jnp.dot(weights[...], cols, preferred_element_type=F32)
            for j in range(CHUNK):
                y = y0 + j
                own = turned[y].astype(F32)
                total = got[0:192, j * 128 : (j + 1) * 128]
                base[x, y] = scale[y : y + 1] * (total + alpha[y : y + 1] * own)
            t = got[192:480]
            lanes = slice(y0 * 128, (y0 + CHUNK) * 128)
            if x < cx - 1:
                tx0[x + 1, :, lanes] = t[0:48].astype(BF16)
            if x > 0:
                tx1[x, :, lanes] = t[48:96].astype(BF16)
            top = min(y0 + CHUNK, 15) - y0
            ty2[x, :, y0 * 128 + 128 : (y0 + top) * 128 + 128] = t[96:144, : top * 128].astype(BF16)
            low = max(y0, 1)
            ty3[x, :, low * 128 : (y0 + CHUNK) * 128] = t[144:192, (low - y0) * 128 :].astype(BF16)
            for j in range(CHUNK):
                at = slice((y0 + j) * 128, (y0 + j + 1) * 128)
                tz4[x, :, at] = shift_lanes(t[192:240, j * 128 : (j + 1) * 128], False).astype(BF16)
                tz5[x, :, at] = shift_lanes(t[240:288, j * 128 : (j + 1) * 128], True).astype(BF16)

    def face(k):
        return slice(192 + ROWS * k, 192 + ROWS * (k + 1))

    def edge_x(k, turned, to):
        for y0 in range(0, 16, CHUNK):
            cols = jnp.concatenate([turned[y0 + j] for j in range(CHUNK)], axis=1)
            got = jnp.dot(weights[face(k)], cols, preferred_element_type=F32)
            to[:, y0 * 128 : (y0 + CHUNK) * 128] = got.astype(BF16)

    def edge_y(k, y, to, at):
        cols = jnp.concatenate([t[y] for t in turned], axis=1)
        got = jnp.dot(weights[face(k)], cols, preferred_element_type=F32).astype(BF16)
        for x in range(cx):
            to[x, :, at : at + 128] = got[:, x * 128 : (x + 1) * 128]

    def service():
        if remote:
            all_a.wait_recv()
            total = slots_a[0]
            for s in range(1, n_plane):
                total = total + slots_a[s]
            part_b[...] = total
            slots_b[line] = total
            send_to_all(in_line, part_b, slots_b.at[line], 1)

    trace_copy.wait()
    adj_copy(0).wait()
    turn(0, turned[0])
    edge_x(1, turned[0], tx1.at[0])
    adj_copy(cx - 1).wait()
    turn(cx - 1, turned[cx - 1])
    edge_x(0, turned[cx - 1], tx0.at[cx])
    for c in (den_copy, met_copy, ids_copy):
        c.wait()

    weighted = den[...] * met[...]
    lane = lax.broadcasted_iota(jnp.int32, (1, 128), 1)
    row = jnp.zeros((1, 128), F32)
    for g in range(GROUPS):
        mine = jnp.sum(jnp.where(ids[...] == g + 1, weighted, 0.0), axis=0)
        mine = jnp.sum(jnp.sum(mine, axis=0, keepdims=True), axis=1, keepdims=True)
        row = row + jnp.where(lane == g, mine, 0.0)
    part_a[...] = row
    if remote:
        slots_a[spot] = row

    if remote:
        pl.semaphore_wait(barrier, n_plane + n_line)
        send_to_all(in_plane, part_a, slots_a.at[spot], 0)
        x_down.start()
        x_up.start()
    for x in (0, cx - 1, 2, 1):
        vel_copy(x).start()
    orient_copy.start()
    lift_copy.start()
    for x in (2, 1):
        adj_copy(x).wait()
        turn(x, turned[x])
    edge_y(3, 0, ty3, 0)
    edge_y(2, 15, ty2, 2048)
    if remote:
        @pl.when(span > 0)
        def _():
            y_down.start()

        @pl.when(span < n_span - 1)
        def _():
            y_up.start()

    vol_copy.wait()
    weights[0:192, :] = vol[...].T
    traces(0, turned[0])
    traces(cx - 1, turned[cx - 1])
    vel_copy(0).wait()
    vel_copy(cx - 1).wait()
    traces(2, turned[2])
    sense(0)
    sense(cx - 1)
    vel_copy(2).wait()
    vel_copy(1).wait()
    traces(1, turned[1])
    sense(2)
    sense(1)
    lift_copy.wait()
    lift_weights[...] = lift[...].T
    orient_copy.wait()
    sign[...] = 1.0 - 2.0 * orient[...].astype(F32)
    if remote:
        s_down.start()
        s_up.start()

        @pl.when(span > 0)
        def _():
            q_down.start()

        @pl.when(span < n_span - 1)
        def _():
            q_up.start()

    service()

    @pl.when(span == 0)
    def _():
        for x in range(cx):
            ty2[x, :, 0:128] = jnp.zeros((ROWS, 128), BF16)
        sy_lo[...] = jnp.zeros_like(sy_lo)

    @pl.when(span == n_span - 1)
    def _():
        for x in range(cx):
            ty3[x, :, 2048:2176] = jnp.zeros((ROWS, 128), BF16)
        sy_hi[...] = jnp.zeros_like(sy_hi)

    if remote:
        @pl.when(span > 0)
        def _():
            y_up.wait_recv()

        @pl.when(span < n_span - 1)
        def _():
            y_down.wait_recv()

    def lifted(x, back, chosen=tuple(range(6)), last=True):
        if len(chosen) == 6:
            block = lift_weights[...]
        else:
            block = jnp.concatenate([lift[ROWS * k : ROWS * (k + 1)] for k in chosen], axis=0).T
        for y0 in range(0, 16, CHUNK):
            lanes = slice(y0 * 128, (y0 + CHUNK) * 128)
            later = slice(y0 * 128 + 128, (y0 + CHUNK) * 128 + 128)
            faces = ((tx0, x, lanes), (tx1, x + 1, lanes), (ty2, x, lanes), (ty3, x, later), (tz4, x, lanes), (tz5, x, lanes))
            parts = []
            for k in chosen:
                ref, at, cut = faces[k]
                rows = [jnp.broadcast_to(sign[k, x, y0 + j : y0 + j + 1], (ROWS, 128)) for j in range(CHUNK)]
                parts.append(ref[at, :, cut] * jnp.concatenate(rows, axis=1).astype(BF16))
            got = jnp.dot(block, jnp.concatenate(parts, axis=0), preferred_element_type=F32)
            for j in range(CHUNK):
                total = base[x, y0 + j] + got[:, j * 128 : (j + 1) * 128]
                if last:
                    back[y0 + j] = total.astype(BF16)
                else:
                    base[x, y0 + j] = total

    def turn_back(x, back):
        for d in range(0, 192, 16):
            held[d : d + 16, x] = jnp.swapaxes(back[:, d : d + 16], 0, 1)

    lifted(1, back_a)
    lifted(2, back_b)
    turn_back(1, back_a)
    core = lax.rem(stream, 2)
    soon = (1 - core) * (cx - 1)
    late = core * (cx - 1)
    if remote:
        @pl.when(core == 0)
        def _():
            x_down.wait_recv()

        @pl.when(core == 1)
        def _():
            x_up.wait_recv()

    lifted(soon, back_a)
    turn_back(2, back_b)
    turn_back(soon, back_a)

    @pl.when(core == 0)
    def _():
        lifted(0, back_b, (1, 2, 3, 4, 5), False)
        if remote:
            x_up.wait_recv()
        lifted(0, back_b, (0,))

    @pl.when(core == 1)
    def _():
        lifted(cx - 1, back_b, (0, 2, 3, 4, 5), False)
        if remote:
            x_down.wait_recv()
        lifted(cx - 1, back_b, (1,))

    turn_back(late, back_b)

    if remote:
        @pl.when(span > 0)
        def _():
            q_up.wait_recv()

        @pl.when(span < n_span - 1)
        def _():
            q_down.wait_recv()

        s_down.wait_recv()
        s_up.wait_recv()
    else:
        for r in (sx_lo, sx_hi, sy_lo, sy_hi):
            r[...] = jnp.zeros_like(r)

    for x in range(cx):
        own = sens[x]
        below_x = sx_lo[...] if x == 0 else sens[x - 1]
        above_x = sx_hi[...] if x == cx - 1 else sens[x + 1]
        beside = below_x + above_x
        beside = beside + shift_rows(own, sy_lo[x : x + 1], False) + shift_rows(own, sy_hi[x : x + 1], True)
        beside = beside + shift_lanes(own, False) + shift_lanes(own, True)
        filt[x] = (own + FILTER_BETA * beside) / (1.0 + 6.0 * FILTER_BETA)

    if remote:
        @pl.when(span > 0)
        def _():
            y_down.wait_send()
            q_down.wait_send()

        @pl.when(span < n_span - 1)
        def _():
            y_up.wait_send()
            q_up.wait_send()

        s_down.wait_send()
        s_up.wait_send()
        x_down.wait_send()
        x_up.wait_send()

    if remote:
        all_b.wait_recv()
        volumes = slots_b[0]
        for s in range(1, n_line):
            volumes = volumes + slots_b[s]
        vol_out[...] = volumes * (1.0 / (den.shape[0] * den.shape[1] * den.shape[2]))
        all_a.wait_send()
        all_b.wait_send()
    else:
        vol_out[...] = part_a[...]


def second_kernel(held, filt_in, vol_in, res_hbm, filt, vol_out, out_sem):
    pieces = out_sem.shape[0]
    step = held.shape[0] // pieces
    copies = [
        pltpu.make_async_copy(held.at[pl.ds(i * step, step)], res_hbm.at[pl.ds(i * step, step)], out_sem.at[i])
        for i in range(pieces)
    ]
    for c in copies:
        c.start()
    filt[...] = filt_in[...]
    for g in range(GROUPS):
        vol_out[g] = vol_in[0, g]
    for c in copies:
        c.wait()


def in_hbm(array):
    return pltpu.with_memory_space_constraint(array, pltpu.HBM)


def shards(
    n_stream, n_span, remote,
    adjoint, velocity, density, metric, orientation, design_ids, volume_block, face_trace, face_lift
):
    cx = adjoint.shape[1]
    hbm_spec = pl.BlockSpec(memory_space=pltpu.HBM)
    vmem_spec = pl.BlockSpec(memory_space=pltpu.VMEM)
    dma = pltpu.SemaphoreType.DMA
    lift_rows = jnp.swapaxes(face_lift, 1, 2).reshape(288, 192)
    whole = (adjoint, velocity, density, metric, design_ids, orientation, volume_block, face_trace.reshape(288, 192), lift_rows)
    cells = (cx, 16, 128)
    dofs = (192, cx, 16, 128)
    mids = [(dofs, BF16), (cells, F32), ((1, 128), F32)]
    n_plane, n_line = PLANE * n_span, n_stream // PLANE
    mid = pl.pallas_call(
        functools.partial(first_kernel, n_stream, n_span, remote),
        out_shape=[pltpu.VMEM(s, d) for s, d in mids],
        in_specs=[hbm_spec] * len(whole),
        out_specs=[vmem_spec] * len(mids),
        scratch_shapes=[
            pltpu.VMEM(dofs, BF16),
            pltpu.VMEM(dofs, BF16),
            pltpu.VMEM(cells, F32),
            pltpu.VMEM(cells, F32),
            pltpu.VMEM(cells, jnp.int32),
            pltpu.VMEM((6, *cells), jnp.int32),
            pltpu.VMEM((192, 192), BF16),
            pltpu.VMEM((288, 192), BF16),
            pltpu.VMEM((480, 192), BF16),
            pltpu.VMEM((192, 288), BF16),
            pltpu.VMEM((6, *cells), F32),
            *[pltpu.VMEM((16, 192, 128), BF16)] * 6,
            pltpu.VMEM((cx, 16, 192, 128), F32),
            pltpu.VMEM((cx + 1, ROWS, 2048), BF16),
            pltpu.VMEM((cx + 1, ROWS, 2048), BF16),
            pltpu.VMEM((cx, ROWS, 2176), BF16),
            pltpu.VMEM((cx, ROWS, 2176), BF16),
            pltpu.VMEM((cx, ROWS, 2048), BF16),
            pltpu.VMEM((cx, ROWS, 2048), BF16),
            pltpu.VMEM(cells, F32),
            pltpu.VMEM((16, 128), F32),
            pltpu.VMEM((16, 128), F32),
            pltpu.VMEM((8, 128), F32),
            pltpu.VMEM((8, 128), F32),
            pltpu.VMEM((8, 128), F32),
            pltpu.VMEM((8, 128), F32),
            pltpu.VMEM((n_plane, 1, 128), F32),
            pltpu.VMEM((max(n_line, 1), 1, 128), F32),
            pltpu.VMEM((1, 128), F32),
            pltpu.VMEM((1, 128), F32),
            dma((cx,)), dma((cx,)), dma((7,)), dma((8,)), dma((8,)), dma((2,)), dma((2,)),
        ],
        compiler_params=pltpu.CompilerParams(
            collective_id=0 if remote else None, has_side_effects=True, vmem_limit_bytes=44 * 2**20
        ),
    )(*[in_hbm(a) for a in whole])
    return pl.pallas_call(
        second_kernel,
        out_shape=[
            jax.ShapeDtypeStruct(adjoint.shape, BF16),
            jax.ShapeDtypeStruct(cells, F32),
            jax.ShapeDtypeStruct((GROUPS,), F32),
        ],
        in_specs=[vmem_spec] * len(mids),
        out_specs=[hbm_spec, vmem_spec, pl.BlockSpec(memory_space=pltpu.SMEM)],
        scratch_shapes=[dma((8,))],
        compiler_params=pltpu.CompilerParams(vmem_limit_bytes=4 * 2**20),
    )(*[pltpu.with_memory_space_constraint(m, pltpu.VMEM) for m in mid])


def solution(mesh, remote=True):
    cells = P("stream", "span", None)
    dofs = P(None, "stream", "span", None)
    return jax.shard_map(
        functools.partial(shards, mesh.shape["stream"], mesh.shape["span"], remote),
        mesh=mesh,
        in_specs=(dofs, dofs, cells, cells, dofs, cells, P(), P(), P()),
        out_specs=(dofs, cells, P()),
        check_vma=False,
    )
```
